128 devices in a mesh: gx: 8 (over z, core), gy: 16 (over y, x).
Axes of the slice: x: 4, y: 4, z: 4, core: 2. Of those that a mesh axis runs over, the one named last changes fastest.
Arguments:
- old_state: bfloat16 [16384, 19, 128], P(('gx', 'gy')), may hold values from -6 to 6
- send_block: int32 [128, 768], P(('gx', 'gy')), may hold values from 0 to 127
- receive_slot_table: int32 [16384, 3], P(('gx', 'gy')), may hold values from 0 to 767, as said below
- interpolation_weight_tiles: bfloat16 [16384, 3, 128, 128], P(('gx', 'gy')), may hold values from -0.3125 to 0.3125
- velocity: float32 [3, 9, 128, 2048], P(None, None, 'gx', 'gy'), may hold values from -6 to 6
- node_mass: float32 [9, 128, 2048], P(None, 'gx', 'gy'), may hold values from 0.5 to 2
- spot_x: int32 [36], replicated, may hold values from 0 to 127
- spot_y: int32 [36], replicated, may hold values from 0 to 2047
Outputs:
- final_state: float32 [19, 8, 128, 2048], P(None, None, 'gx', 'gy')
- final_velocity: float32 [3, 9, 128, 2048], P(None, None, 'gx', 'gy')
The draws below stay inside these ranges and needn't reach their ends.
Inputs may be any that keep to these rules, and one draw needn't show every extreme that they name: `receive_slot_table`: the 384 entries of one device's new blocks name distinct slots; so at most 6 of them come from one source device, and for every device some source device supplies exactly 6.
All inputs are finite; a program needn't handle non-finite values.
Results may differ from the reference program's by a relative error of at most 0.0003.
Values may be sent and summed in bfloat16 or wider, within the bound.
A program may use at most 64 MiB of HBM per device.

```python
import math
import jax
import jax.numpy as jnp
from jax import lax

EX = 16
EY = 128
EZ = 8
COMPS = 19
K = 3
SPOTS = 36
STEPS = 2
NB = 128
CAP = 6
TOTAL_BLOCKS = 16384
NXE = 128
NYE = 2048
N_GX = 8
N_GY = 16
DEVICES = 128


def draw_receive_slot_table(key, part):
    slot_count = DEVICES * CAP
    entries = NB * K
    base = jax.random.fold_in(key, 31)

    def for_target(target):
        first_key = jax.random.fold_in(base, target)
        second_key = jax.random.fold_in(first_key, 1)
        ranking = jax.random.permutation(first_key, slot_count)
        slot_ids = jnp.arange(slot_count, dtype=jnp.int32)
        forced = slot_ids // CAP == (target + 1) % DEVICES
        score = jnp.where(forced, ranking - slot_count, ranking)
        ordered = jnp.argsort(score)
        chosen = jax.random.permutation(second_key, ordered[:entries])
        return chosen.reshape(NB, K)
    table = jax.vmap(for_target)(jnp.arange(DEVICES, dtype=jnp.int32))
    return table.reshape(DEVICES * NB, K).astype(jnp.int32)


def set_ends(array, stream_key, smallest, high):
    place = [jax.random.randint(jax.random.fold_in(stream_key, axis), (), 0, length) for axis, length in enumerate(array.shape)]
    longest = array.shape.index(max(array.shape))
    beside = place[:longest] + [(place[longest] + 1) % array.shape[longest]] + place[longest + 1:]
    return array.at[tuple(place)].set(smallest).at[tuple(beside)].set(high)


def block_scale(stream_key, extent, shards, least, top_value):
    factor_of, own = 1.0, jax.random.fold_in(stream_key, 6)
    for dim, shards_of in shards:
        steps = jnp.exp(jax.random.uniform(jax.random.fold_in(own, dim), (shards_of,), jnp.float32, least / len(shards), top_value / len(shards)))
        factor_of = factor_of * jnp.repeat(steps, extent[dim] // shards_of).reshape([-1 if axis == dim else 1 for axis in range(len(extent))])
    return factor_of


def normal_values(stream_key, extent, deviation, reach, split=(), held_as=jnp.bfloat16):
    level = block_scale(stream_key, extent, split, -0.22, 0.18) if split else 1.0
    drawn = jax.random.normal(stream_key, extent, jnp.float32) * deviation * level
    return jnp.minimum(jnp.maximum(drawn, -reach), reach).astype(held_as)


def setup_inputs(seed: int = 0) -> dict:
    key_of = jax.random.split(jax.random.key(seed), 9)
    return {
        "old_state": normal_values(key_of[0], (TOTAL_BLOCKS, COMPS, EY), 1.0, 6.0, ((0, 128),)),
        "send_block": set_ends(jax.random.randint(key_of[1], (DEVICES, DEVICES * CAP), 0, NB), jax.random.fold_in(key_of[1], 1), 0, NB - 1).astype(jnp.int32),
        "receive_slot_table": draw_receive_slot_table(jax.random.fold_in(key_of[8], 71), 0),
        "interpolation_weight_tiles": normal_values(key_of[3], (TOTAL_BLOCKS, K, EY, EY), (K * EY) ** -0.5, 0.3125, ((0, 128),)),
        "velocity": normal_values(key_of[4], (3, EZ + 1, NXE, NYE), 1.0, 6.0, ((2, 8), (3, 16)), jnp.float32),
        "node_mass": jnp.clip(jnp.exp(math.log(2.0) - 1.3862944 * jax.random.uniform(key_of[5], (EZ + 1, NXE, NYE), jnp.float32) ** block_scale(key_of[5], (EZ + 1, NXE, NYE), ((1, 8), (2, 16)), -0.2, 0.2)), 0.5, 2.0),
        "spot_x": set_ends(jax.random.randint(key_of[6], (SPOTS,), 0, NXE), jax.random.fold_in(key_of[6], 1), 0, NXE - 1).astype(jnp.int32),
        "spot_y": set_ends(jax.random.randint(key_of[7], (SPOTS,), 0, NYE), jax.random.fold_in(key_of[7], 1), 0, NYE - 1).astype(jnp.int32),
    }


SHEAR = 1.0
BULK = 2.0
YIELD_STRESS = 2.0
HARD_ISO = 0.3
HARD_KIN = 0.5
TIME_STEP = 0.2
PEAK_PRESSURE = 1.5
RADIUS_SQUARED = 36.0

def zsum(field):
    return field[:, :-1] + field[:, 1:]

def element_update(state, corner_00, corner_01, corner_10, corner_11):
    grad_x = 0.25 * zsum(corner_10 + corner_11 - corner_00 - corner_01)
    grad_y = 0.25 * zsum(corner_01 + corner_11 - corner_00 - corner_10)
    every = corner_00 + corner_01 + corner_10 + corner_11
    grad_z = 0.25 * (every[:, 1:] - every[:, :-1])
    strain = [TIME_STEP * grad_x[0], TIME_STEP * grad_y[1], TIME_STEP * grad_z[2], TIME_STEP * 0.5 * (grad_y[0] + grad_x[1]), TIME_STEP * 0.5 * (grad_z[1] + grad_y[2]), TIME_STEP * 0.5 * (grad_x[2] + grad_z[0])]
    trace = strain[0] + strain[1] + strain[2]
    lame = BULK - 2.0 * SHEAR / 3.0
    trial = []
    for index in range(6):
        value = state[index] + 2.0 * SHEAR * strain[index]
        if index < 3:
            value = value + lame * trace
        trial.append(value)
    mean_value = (trial[0] + trial[1] + trial[2]) / 3.0
    deviator = []
    for index in range(6):
        shifted = trial[index] - mean_value if index < 3 else trial[index]
        deviator.append(shifted - state[6 + index])
    norm_two = deviator[0] ** 2 + deviator[1] ** 2 + deviator[2] ** 2 + 2.0 * (deviator[3] ** 2 + deviator[4] ** 2 + deviator[5] ** 2)
    equiv = jnp.sqrt(1.5 * norm_two)
    epbar = state[18]
    excess = jnp.maximum(equiv - (YIELD_STRESS + HARD_ISO * epbar), 0.0)
    dgamma = excess / (3.0 * SHEAR + HARD_ISO + HARD_KIN)
    factor = dgamma / jnp.maximum(equiv, YIELD_STRESS)
    stress = [trial[index] - 3.0 * SHEAR * factor * deviator[index] for index in range(6)]
    back = [state[6 + index] + HARD_KIN * factor * deviator[index] for index in range(6)]
    plastic = [state[12 + index] + 1.5 * factor * deviator[index] for index in range(6)]
    new_state = jnp.stack(stress + back + plastic + [epbar + dgamma])
    along_x = -0.25 * jnp.stack([stress[0], stress[3], stress[5]])
    along_y = -0.25 * jnp.stack([stress[3], stress[1], stress[4]])
    along_z = -0.25 * jnp.stack([stress[5], stress[4], stress[2]])
    zero_layer = jnp.zeros_like(along_z[:, :1])
    corner_forces = []
    for sign_a in (-1.0, 1.0):
        for sign_b in (-1.0, 1.0):
            sideways_neighbour = sign_a * along_x + sign_b * along_y
            lower = jnp.concatenate([sideways_neighbour - along_z, zero_layer], axis=1)
            upper = jnp.concatenate([zero_layer, sideways_neighbour + along_z], axis=1)
            corner_forces.append(lower + upper)
    return (new_state, corner_forces)

def pressure_field(spot_x, spot_y, xs, ys):
    factor_x = jnp.exp(-(xs[None, :] - spot_x.astype(jnp.float32)[:, None]) ** 2 / RADIUS_SQUARED)
    factor_y = jnp.exp(-(ys[None, :] - spot_y.astype(jnp.float32)[:, None]) ** 2 / RADIUS_SQUARED)
    return jnp.dot(factor_x.T, factor_y, precision=lax.Precision.HIGHEST)

def reference(old_state, send_block, receive_slot_table, interpolation_weight_tiles, velocity, node_mass, spot_x, spot_y):
    devices = N_GX * N_GY

    def remap_one(target):
        slots = lax.dynamic_slice_in_dim(receive_slot_table, (target * NB).astype(jnp.int32), NB, 0)
        sources = slots // CAP
        column = target * CAP + slots % CAP
        local = send_block[sources, column]
        element_row_list = old_state[sources * NB + local].astype(jnp.float32)
        weight_tile_stack = lax.dynamic_slice_in_dim(interpolation_weight_tiles, (target * NB).astype(jnp.int32), NB, 0).astype(jnp.float32)
        return jnp.einsum('fylt,fyat->lfa', element_row_list, weight_tile_stack)
    blocks = lax.map(remap_one, jnp.arange(devices, dtype=jnp.int32))
    blocks = blocks.reshape(N_GX, N_GY, COMPS, EZ, EX, EY)
    state = blocks.transpose(2, 3, 0, 4, 1, 5).reshape(COMPS, EZ, NXE, NYE)
    xs = jnp.arange(NXE, dtype=jnp.int32).astype(jnp.float32)
    ys = jnp.arange(NYE, dtype=jnp.int32).astype(jnp.float32)
    pressure = pressure_field(spot_x, spot_y, xs, ys)
    for step_index in range(STEPS):
        padded = jnp.pad(velocity, ((0, 0), (0, 0), (0, 1), (0, 1)))
        corner_00 = padded[:, :, 0:NXE, 0:NYE]
        corner_01 = padded[:, :, 0:NXE, 1:NYE + 1]
        corner_10 = padded[:, :, 1:NXE + 1, 0:NYE]
        corner_11 = padded[:, :, 1:NXE + 1, 1:NYE + 1]
        state, corner_forces = element_update(state, corner_00, corner_01, corner_10, corner_11)
        forces = jnp.zeros((3, EZ + 1, NXE + 1, NYE + 1), jnp.float32)
        forces = forces.at[:, :, 0:NXE, 0:NYE].add(corner_forces[0])
        forces = forces.at[:, :, 0:NXE, 1:NYE + 1].add(corner_forces[1])
        forces = forces.at[:, :, 1:NXE + 1, 0:NYE].add(corner_forces[2])
        forces = forces.at[:, :, 1:NXE + 1, 1:NYE + 1].add(corner_forces[3])
        forces = forces[:, :, :NXE, :NYE]
        forces = forces.at[2, EZ].add(-PEAK_PRESSURE * pressure)
        velocity = velocity + TIME_STEP * forces / node_mass[None]
    return (state, velocity)
```

```python
import jax
import jax.numpy as jnp
from jax import lax
from jax.experimental import pallas as pl
from jax.experimental.pallas import tpu as pltpu
from jax.sharding import PartitionSpec as P

SHEAR = 1.0
BULK = 2.0
YIELD_STRESS = 2.0
HARD_ISO = 0.3
HARD_KIN = 0.5
TIME_STEP = 0.2
PEAK_PRESSURE = 1.5
RADIUS_SQUARED = 36.0

MESH = pl.DeviceIdType.MESH
F32 = jnp.float32
BF16 = jnp.bfloat16

GROUPS = ((0, 7, "x", "y", "z"), (7, 6, "y", "z", "x"), (13, 6, "z", "x", "y"))
DIM = {"z": 0, "y": 2, "x": 3}
SPOTS = 36
NODES = 27


def iota(shape, dim):
    return lax.broadcasted_iota(jnp.int32, shape, dim)


def kernel(
    old, idx, ridx, w, vel, mass, spot_x, spot_y,
    st, vout,
    h0, h1, h2, s0, s1, s2, u0, u1, u2, g0, g1, g2,
    ibuf, psel, qsel, xs, wv, rem,
    vext, vcol, dtm, dtmc, press, pressc, ddx, ddy, dsm, s6, fm, cl, cr,
    rowpack, rowin, colpack, colin, corin,
    row_up, row_dn, row_up_in, row_dn_in, cl_in, cr_in, diag_in,
    cr2, row2, cr2_in, row2_in, diag2_in,
    p1_s, p1_r, ix_s, ix_r, p2_s, p2_r, p3_s, p3_r, loc1, loc2, loc3, wsem,
    hs, hr, e1_s, e1_r, e2_s, e2_r,
):
    hbuf, sbuf, ubuf, gbuf = (h0, h1, h2), (s0, s1, s2), (u0, u1, u2), (g0, g1, g2)
    di = lax.axis_index("gx")
    dj = lax.axis_index("gy")
    here = {"z": di // 2, "c": di % 2, "y": dj // 4, "x": dj % 4}

    def device(**moved):
        at = dict(here)
        for axis, step in moved.items():
            size = 2 if axis == "c" else 4
            at[axis] = (at[axis] + step) % size
        return (at["z"] * 2 + at["c"], at["y"] * 4 + at["x"])

    def plate(a, b):
        return ((di + a + 8) % 8, (dj + b + 16) % 16)

    around = [(a, b) for a in (-1, 0, 1) for b in (-1, 0, 1) if (a, b) != (0, 0)]
    partners = [device(**{axis: d, "c": c}) for axis in "xyz" for d in (1, 2, 3) for c in (0, 1)]
    partners.append(device(c=1))
    partners += [plate(a, b) for a, b in around]
    barrier = pltpu.get_barrier_semaphore()
    for partner in partners:
        pl.semaphore_signal(barrier, inc=1, device_id=partner, device_id_type=MESH)

    def remote(src, dst, ssem, rsem, target):
        return pltpu.make_async_remote_copy(
            src_ref=src, dst_ref=dst, send_sem=ssem, recv_sem=rsem, device_id=target, device_id_type=MESH
        )

    local1 = []
    for q, (first, count, ga, pa, qa) in enumerate(GROUPS):
        mine = here[ga]
        local1.append((
            pltpu.make_async_copy(old.at[pl.ds(first, count)], hbuf[q].at[mine], loc1.at[q, 0]),
            pltpu.make_async_copy(idx.at[q, mine], ibuf.at[q, mine], loc1.at[q, 1]),
        ))
        for copy in local1[-1]:
            copy.start()
    pl.semaphore_wait(barrier, len(partners))

    phase1 = []
    for d in (1, 2, 3):
        for q, (first, count, ga, pa, qa) in enumerate(GROUPS):
            mine = here[ga]
            target = device(**{ga: d})
            tg = (mine + d) % 4
            pair = (
                remote(idx.at[q, tg], ibuf.at[q, mine], ix_s.at[q, d - 1], ix_r.at[q, d - 1], target),
                remote(old.at[pl.ds(first, count)], hbuf[q].at[mine], p1_s.at[q, d - 1], p1_r.at[q, d - 1], target),
            )
            for copy in pair:
                copy.start()
            phase1.append((q, pair))

    weights = [
        pltpu.make_async_copy(w.at[pl.ds(n * 32, 32)], wv.at[pl.ds(n * 32, 32)], wsem.at[n]) for n in range(4)
    ]
    for copy in weights:
        copy.start()

    lane16 = iota((16, 128), 1)
    packed = jnp.zeros((16, 128), F32)
    for n in range(NODES):
        plane = vel[n]
        rowpack[n:n + 1, :] = plane[0:1, :]
        moved = plane if n == 0 else pltpu.roll(plane, n, 1)
        packed = jnp.where(lane16 == n, moved, packed)
        heavy = pltpu.roll(mass[n % 9], n + 32, 1)
        packed = jnp.where(lane16 == n + 32, heavy, packed)
    colpack[...] = packed
    for n in range(9):
        rowpack[32 + n:33 + n, :] = mass[n, 0:1, :]
    halo = (
        remote(rowpack, rowin, hs.at[0], hr.at[0], plate(-1, 0)),
        remote(colpack, colin, hs.at[1], hr.at[1], plate(0, -1)),
        remote(colpack.at[pl.ds(0, 8)], corin, hs.at[2], hr.at[2], plate(-1, -1)),
    )
    for copy in halo:
        copy.start()

    ridx_t = jnp.transpose(ridx[...])
    for q in range(3):
        for k in range(3):
            column = ridx_t[:, q * 3 + k:q * 3 + k + 1]
            for m in range(6):
                hit = column == (iota((128, 128), 1) + m * 128).astype(F32)
                qsel[q, k * 128:(k + 1) * 128, m * 128:(m + 1) * 128] = jnp.where(hit, 1.0, 0.0).astype(BF16)

    row24 = iota((24, 128), 0)
    lane24 = iota((24, 128), 1)
    node_x = (di * 16 + row24).astype(F32)
    node_y = (dj * 128 + lane24).astype(F32)
    next_y = (dj * 128 + 128).astype(F32)

    def spot(n, sums):
        main, side = sums
        sx = spot_x[n].astype(F32)
        sy = spot_y[n].astype(F32)
        far_x = (node_x - sx) ** 2
        main = main + jnp.exp(-(far_x + (node_y - sy) ** 2) / RADIUS_SQUARED)
        side = side + jnp.exp(-(far_x + (next_y - sy) ** 2) / RADIUS_SQUARED)
        return (main, side)

    main, side = lax.fori_loop(0, SPOTS, spot, (jnp.zeros((24, 128), F32), jnp.zeros((24, 128), F32)))
    press[...] = -PEAK_PRESSURE * main
    pressc[...] = jnp.where(lane24 == NODES - 1, -PEAK_PRESSURE * side, 0.0)

    phase2 = []
    for q, (first, count, ga, pa, qa) in enumerate(GROUPS):
        for copy in local1[q]:
            copy.wait()
        for of, pair in phase1:
            if of == q:
                for copy in pair:
                    copy.wait_recv()
        table = jnp.concatenate([ibuf[q].reshape(32, 128), jnp.zeros((96, 128), F32)], axis=0)
        table_t = jnp.transpose(table)
        lanes = iota((128, 128), 1).astype(F32)
        for sg in range(4):
            for rc in range(6):
                hit = table_t[:, sg * 8 + rc:sg * 8 + rc + 1] == lanes
                psel[rc * 128:(rc + 1) * 128, sg * 128:(sg + 1) * 128] = jnp.where(hit, 1.0, 0.0).astype(BF16)
        for half in range(2):
            pick = psel[half * 384:(half + 1) * 384, :]
            for comp in range(count):
                blocks = hbuf[q][:, comp].reshape(512, 128)
                rows = jnp.dot(pick, blocks, preferred_element_type=F32)
                for t in range(16):
                    sbuf[q][half * 2 + t // 8, t % 8, :, comp * 128:(comp + 1) * 128] = rows[
                        t * 24:(t + 1) * 24
                    ].astype(BF16)
        mine = here[pa]
        own = pltpu.make_async_copy(sbuf[q].at[mine], ubuf[q].at[mine], loc2.at[q])
        own.start()
        copies = [
            remote(sbuf[q].at[(mine + d) % 4], ubuf[q].at[mine], p2_s.at[q, d - 1], p2_r.at[q, d - 1], device(**{pa: d}))
            for d in (1, 2, 3)
        ]
        for copy in copies:
            copy.start()
        phase2.append((own, copies))

    for copy in halo:
        copy.wait_recv()
    low_i, high_i = (di > 0).astype(F32), (di < 7).astype(F32)
    low_j, high_j = (dj > 0).astype(F32), (dj < 15).astype(F32)
    first8 = iota((8, 128), 0) == 0
    row_mask = jnp.where(row24 < 16, 1.0, high_i)
    for n in range(NODES):
        vext[n, 0:16, :] = vel[n]
        vext[n, 16:24, :] = jnp.where(first8, rowin[n:n + 1, :] * high_i, 0.0)
    for n in range(9):
        dtm[n, 0:16, :] = TIME_STEP / mass[n]
        dtm[n, 16:24, :] = jnp.where(first8, high_i * TIME_STEP / rowin[32 + n:33 + n, :], 0.0)
    column = jnp.concatenate([colin[...], jnp.where(first8, corin[...] * high_i, 0.0)], axis=0)
    vcol[...] = jnp.where(lane24 < NODES, column * high_j, 0.0)
    heavy = pltpu.roll(jnp.concatenate([colin[...], corin[...]], axis=0), 96, 1)
    used = (lane24 < NODES) & (row24 < 17)
    dtmc[...] = jnp.where(used, high_j * row_mask * TIME_STEP / jnp.where(used, heavy, 1.0), 0.0)

    def differences():
        edge = lane24 == 127
        for n in range(NODES):
            v = vext[n]
            right = jnp.where(edge, vcol[:, n:n + 1], pltpu.roll(v, 127, 1))
            total = v + right
            delta = right - v
            total_up = pltpu.roll(total, 23, 0)
            delta_up = pltpu.roll(delta, 23, 0)
            ddx[n] = (total_up - total)[0:16]
            ddy[n] = (delta_up + delta)[0:16]
            dsm[n] = (total_up + total)[0:16]

    differences()
    for comp in range(6):
        s6[comp, 0] = jnp.zeros((16, 128), F32)
        s6[comp, 9] = jnp.zeros((16, 128), F32)

    phase3 = []
    for q, (first, count, ga, pa, qa) in enumerate(GROUPS):
        own, copies = phase2[q]
        own.wait()
        for copy in copies:
            copy.wait_recv()
        mine = here[qa] * 2 + here["c"]
        own = pltpu.make_async_copy(ubuf[q].at[:, mine], gbuf[q].at[mine], loc3.at[q])
        own.start()
        copies = []
        for d in (2, 1, 3, 0):
            for c in (0, 1):
                if (d, c) != (0, 0):
                    there = ((here[qa] + d) % 4) * 2 + (here["c"] + c) % 2
                    slot = d * 2 + c - 1
                    copies.append(remote(
                        ubuf[q].at[:, there], gbuf[q].at[mine], p3_s.at[q, slot], p3_r.at[q, slot], device(**{qa: d, "c": c})
                    ))
        for copy in copies:
            copy.start()
        phase3.append((own, copies))

    for q, (first, count, ga, pa, qa) in enumerate(GROUPS):
        own, copies = phase3[q]
        own.wait()
        for copy in copies:
            copy.wait_recv()
        for comp in range(count):
            rows = gbuf[q][:, :, :, comp * 128:(comp + 1) * 128].astype(F32).reshape(768, 128).astype(BF16)
            xs[pl.ds(first + comp, 384, stride=24), :] = jnp.dot(qsel[q], rows, preferred_element_type=F32)

    for copy in weights:
        copy.wait()

    def block(g, carry):
        total = jnp.zeros((24, 128), F32)
        for k in range(3):
            start = pl.multiple_of((k * 128 + g) * 24, 8)
            part = xs[pl.ds(start, 24), :].astype(BF16)
            total = total + lax.dot_general(part, wv[g, k], (((1,), (1,)), ((), ())), preferred_element_type=F32)
        rem[pl.ds(pl.multiple_of(g * 24, 8), 24), :] = total
        return carry

    lax.fori_loop(0, 128, block, 0, unroll=4)

    def elements(step):
        def layer(z, carry):
            def state(n):
                if step == 0:
                    return rem[pl.ds(z * 384 + n, 16, stride=24), :]
                return st[n, z]

            gx = [0.25 * (ddx[n * 9 + z] + ddx[n * 9 + z + 1]) for n in range(3)]
            gy = [0.25 * (ddy[n * 9 + z] + ddy[n * 9 + z + 1]) for n in range(3)]
            gz = [0.25 * (dsm[n * 9 + z + 1] - dsm[n * 9 + z]) for n in range(3)]
            strain = [
                TIME_STEP * gx[0],
                TIME_STEP * gy[1],
                TIME_STEP * gz[2],
                TIME_STEP * 0.5 * (gy[0] + gx[1]),
                TIME_STEP * 0.5 * (gz[1] + gy[2]),
                TIME_STEP * 0.5 * (gx[2] + gz[0]),
            ]
            trace = strain[0] + strain[1] + strain[2]
            lame = BULK - 2.0 * SHEAR / 3.0
            trial = []
            for n in range(6):
                value = state(n) + 2.0 * SHEAR * strain[n]
                if n < 3:
                    value = value + lame * trace
                trial.append(value)
            mean = (trial[0] + trial[1] + trial[2]) * (1.0 / 3.0)
            back = [state(6 + n) for n in range(6)]
            xi = [(trial[n] - mean if n < 3 else trial[n]) - back[n] for n in range(6)]
            norm = xi[0] ** 2 + xi[1] ** 2 + xi[2] ** 2 + 2.0 * (xi[3] ** 2 + xi[4] ** 2 + xi[5] ** 2)
            equiv = jnp.sqrt(1.5 * norm)
            epbar = state(18)
            excess = jnp.maximum(equiv - (YIELD_STRESS + HARD_ISO * epbar), 0.0)
            dgamma = excess * (1.0 / (3.0 * SHEAR + HARD_ISO + HARD_KIN))
            factor = dgamma / jnp.maximum(equiv, YIELD_STRESS)
            for n in range(6):
                shift = factor * xi[n]
                stress = trial[n] - 3.0 * SHEAR * shift
                plastic = state(12 + n) + 1.5 * shift
                st[n, z] = stress
                s6[n, z + 1] = stress
                st[6 + n, z] = back[n] + HARD_KIN * shift
                st[12 + n, z] = plastic
            st[18, z] = epbar + dgamma
            return carry

        lax.fori_loop(0, 8, layer, 0)

    along = ((0, 3, 5), (3, 1, 4), (5, 4, 2))
    inner = lane16 > 0
    zeros8 = jnp.zeros((8, 128), F32)

    def forces(last):
        right0 = jnp.zeros((16, 128), F32)
        right1 = jnp.zeros((16, 128), F32)
        left = jnp.zeros((24, 128), F32)
        for i in range(3):
            for k in range(9):
                n = i * 9 + k
                ax = -0.25 * (s6[along[0][i], k + 1] + s6[along[0][i], k])
                ay = -0.25 * (s6[along[1][i], k + 1] + s6[along[1][i], k])
                az = -0.25 * (s6[along[2][i], k] - s6[along[2][i], k + 1])
                near, far = az - ax, az + ax
                near_up, far_up = near + ay, far + ay
                roll0, roll1 = pltpu.roll(near_up, 1, 1), pltpu.roll(far_up, 1, 1)
                e0 = near - ay + jnp.where(inner, roll0, 0.0)
                e1 = far - ay + jnp.where(inner, roll1, 0.0)
                turn0 = roll0 if n == 0 else pltpu.roll(near_up, n + 1, 1)
                turn1 = roll1 if n == 0 else pltpu.roll(far_up, n + 1, 1)
                right0 = jnp.where(lane16 == n, turn0, right0)
                right1 = jnp.where(lane16 == n, turn1, right1)
                whole = jnp.concatenate([e0, zeros8], axis=0) + pltpu.roll(jnp.concatenate([e1, zeros8], axis=0), 1, 0)
                fm[n] = whole
                if last:
                    row2[n:n + 1, :] = whole[16:17]
                else:
                    row_up[n:n + 1, :] = whole[16:17]
                    row_dn[n:n + 1, :] = whole[0:1]
                    left = jnp.where(lane24 == n, whole if n == 0 else pltpu.roll(whole, n, 1), left)
        right = jnp.concatenate([right0, zeros8], axis=0) + pltpu.roll(jnp.concatenate([right1, zeros8], axis=0), 1, 0)
        return left, right

    elements(0)
    left, right = forces(False)
    cl[...] = left
    cr[...] = right
    row_up[32:40, :] = right[16:24]
    row_dn[32:40, :] = right[0:8]
    low, high = pl.ds(0, 8), pl.ds(16, 8)
    round1 = (
        remote(row_up, row_up_in, e1_s.at[0], e1_r.at[0], plate(1, 0)),
        remote(row_dn, row_dn_in, e1_s.at[1], e1_r.at[1], plate(-1, 0)),
        remote(cr, cr_in, e1_s.at[2], e1_r.at[2], plate(0, 1)),
        remote(cl, cl_in, e1_s.at[3], e1_r.at[3], plate(0, -1)),
        remote(cr.at[high], diag_in.at[0], e1_s.at[4], e1_r.at[4], plate(1, 1)),
        remote(cr.at[low], diag_in.at[1], e1_s.at[5], e1_r.at[5], plate(-1, 1)),
        remote(cl.at[high], diag_in.at[2], e1_s.at[6], e1_r.at[6], plate(1, -1)),
        remote(cl.at[low], diag_in.at[3], e1_s.at[7], e1_r.at[7], plate(-1, -1)),
    )
    for copy in round1:
        copy.start()
    for copy in round1:
        copy.wait_recv()

    def ends(at_low, at_high):
        return jnp.concatenate([
            jnp.where(first8, at_low * low_i, 0.0), zeros8, jnp.where(first8, at_high * high_i, 0.0)
        ], axis=0)

    add_left = low_j * (cr_in[...] + ends(diag_in[0], diag_in[1]))
    add_right = high_j * (cl_in[...] + ends(diag_in[2], diag_in[3]))
    col_force = cr[...] + add_right + ends(row_up_in[32:40], row_dn_in[32:40]) + pressc[...]
    vcol[...] = vcol[...] + col_force * dtmc[...]
    for n in range(NODES):
        rows = jnp.concatenate([
            jnp.where(first8, row_up_in[n:n + 1] * low_i, 0.0), zeros8, jnp.where(first8, row_dn_in[n:n + 1] * high_i, 0.0)
        ], axis=0)
        force = fm[n] + rows + jnp.where(lane24 == 0, add_left[:, n:n + 1], 0.0)
        if n == NODES - 1:
            force = force + press[...]
        vext[n] = vext[n] + force * dtm[n % 9]

    differences()
    elements(1)
    left, right = forces(True)
    cr2[...] = right
    round2 = (
        remote(row2, row2_in, e2_s.at[0], e2_r.at[0], plate(1, 0)),
        remote(cr2, cr2_in, e2_s.at[1], e2_r.at[1], plate(0, 1)),
        remote(cr2.at[high], diag2_in, e2_s.at[2], e2_r.at[2], plate(1, 1)),
    )
    for copy in round2:
        copy.start()
    for copy in round2:
        copy.wait_recv()
    corner = jnp.concatenate([jnp.where(first8, diag2_in[...] * low_i, 0.0), zeros8], axis=0)
    add_left = low_j * (cr2_in[0:16] + corner)
    for n in range(NODES):
        rows = jnp.concatenate([jnp.where(first8, row2_in[n:n + 1] * low_i, 0.0), zeros8], axis=0)
        force = fm[n, 0:16] + rows + jnp.where(lane16 == 0, add_left[:, n:n + 1], 0.0)
        if n == NODES - 1:
            force = force + press[0:16]
        vout[n] = vext[n, 0:16] + force * dtm[n % 9, 0:16]

    for q, pair in phase1:
        for copy in pair:
            copy.wait_send()
    for own, copies in phase2 + phase3:
        for copy in copies:
            copy.wait_send()
    for copy in halo + round1 + round2:
        copy.wait_send()


def body(
    old_state,
    send_block,
    receive_slot_table,
    interpolation_weight_tiles,
    velocity,
    node_mass,
    spot_x,
    spot_y,
):
    di, dj = lax.axis_index("gx"), lax.axis_index("gy")
    here = {"z": di // 2, "y": dj // 4, "x": dj % 4}
    wanted = send_block.reshape(4, 2, 4, 4, 6).astype(F32)
    asked = receive_slot_table.T
    source, slot = asked // 6, asked % 6
    place = {"z": source // 32, "c": (source // 16) % 2, "y": (source // 4) % 4, "x": source % 4}
    tables, rows = [], []
    for first, count, ga, pa, qa in GROUPS:
        table = wanted.transpose(DIM[ga], DIM[pa], DIM[qa], 1, 4).reshape(4, 32, 1, 6)
        table = jnp.where(jnp.arange(4)[:, None] == here[ga], table, 255.0).reshape(4, 6, 128)
        tables.append(jnp.pad(table, ((0, 0), (0, 2), (0, 0))))
        rows.append(((place[qa] * 2 + place["c"]) * 4 + place[pa]) * 24 + place[ga] * 6 + slot)
    idx = jnp.stack(tables)
    ridx = jnp.pad(jnp.concatenate(rows).astype(F32), ((0, 119), (0, 0)))

    vmem = pl.BlockSpec(memory_space=pltpu.VMEM)
    smem = pl.BlockSpec(memory_space=pltpu.SMEM)
    anywhere = pl.BlockSpec(memory_space=pl.ANY)
    counts = [group[1] for group in GROUPS]
    scratch = (
        [pltpu.VMEM((4, n, 128, 128), BF16) for n in counts]
        + [pltpu.VMEM((4, 8, 24, n * 128), BF16) for n in counts]
        + [pltpu.VMEM((4, 8, 24, n * 128), BF16) for n in counts]
        + [pltpu.VMEM((8, 4, 24, n * 128), BF16) for n in counts]
        + [
            pltpu.VMEM((3, 4, 8, 128), F32),
            pltpu.VMEM((768, 512), BF16),
            pltpu.VMEM((3, 384, 768), BF16),
            pltpu.VMEM((384 * 24, 128), F32),
            pltpu.VMEM((128, 3, 128, 128), BF16),
            pltpu.VMEM((128 * 24, 128), F32),
            pltpu.VMEM((27, 24, 128), F32),
            pltpu.VMEM((24, 128), F32),
            pltpu.VMEM((9, 24, 128), F32),
            pltpu.VMEM((24, 128), F32),
            pltpu.VMEM((24, 128), F32),
            pltpu.VMEM((24, 128), F32),
            pltpu.VMEM((27, 16, 128), F32),
            pltpu.VMEM((27, 16, 128), F32),
            pltpu.VMEM((27, 16, 128), F32),
            pltpu.VMEM((6, 10, 16, 128), F32),
            pltpu.VMEM((27, 24, 128), F32),
            pltpu.VMEM((24, 128), F32),
            pltpu.VMEM((24, 128), F32),
            pltpu.VMEM((48, 128), F32),
            pltpu.VMEM((48, 128), F32),
            pltpu.VMEM((16, 128), F32),
            pltpu.VMEM((16, 128), F32),
            pltpu.VMEM((8, 128), F32),
            pltpu.VMEM((40, 128), F32),
            pltpu.VMEM((40, 128), F32),
            pltpu.VMEM((40, 128), F32),
            pltpu.VMEM((40, 128), F32),
            pltpu.VMEM((24, 128), F32),
            pltpu.VMEM((24, 128), F32),
            pltpu.VMEM((4, 8, 128), F32),
            pltpu.VMEM((24, 128), F32),
            pltpu.VMEM((32, 128), F32),
            pltpu.VMEM((24, 128), F32),
            pltpu.VMEM((32, 128), F32),
            pltpu.VMEM((8, 128), F32),
        ]
        + [
            pltpu.SemaphoreType.DMA(shape)
            for shape in (
                (3, 3), (3, 3), (3, 3), (3, 3), (3, 3), (3, 3), (3, 7), (3, 7), (3, 2), (3,), (3,), (4,),
                (3,), (3,), (8,), (8,), (3,), (3,),
            )
        ]
    )
    state, moved = pl.pallas_call(
        kernel,
        out_shape=(
            jax.ShapeDtypeStruct((19, 8, 16, 128), F32),
            jax.ShapeDtypeStruct((27, 16, 128), F32),
        ),
        in_specs=[anywhere, vmem, vmem, anywhere, vmem, vmem, smem, smem],
        out_specs=(vmem, vmem),
        scratch_shapes=scratch,
        compiler_params=pltpu.CompilerParams(
            collective_id=0, has_side_effects=True, vmem_limit_bytes=56 * 2**20
        ),
        name="remap_and_steps",
    )(
        old_state.transpose(1, 0, 2),
        idx,
        ridx,
        interpolation_weight_tiles,
        velocity.reshape(27, 16, 128),
        node_mass,
        spot_x,
        spot_y,
    )
    return (state, moved.reshape(3, 9, 16, 128))


def solution(mesh):
    return jax.shard_map(
        body,
        mesh=mesh,
        in_specs=(
            P(("gx", "gy"), None, None),
            P(("gx", "gy"), None),
            P(("gx", "gy"), None),
            P(("gx", "gy"), None, None, None),
            P(None, None, "gx", "gy"),
            P(None, "gx", "gy"),
            P(),
            P(),
        ),
        out_specs=(P(None, None, "gx", "gy"), P(None, None, "gx", "gy")),
        check_vma=False,
    )
```

```python
import jax
import jax.numpy as jnp
from jax import lax
from jax.experimental import pallas as pl
from jax.experimental.pallas import tpu as pltpu
from jax.sharding import PartitionSpec as P

SHEAR = 1.0
BULK = 2.0
YIELD_STRESS = 2.0
HARD_ISO = 0.3
HARD_KIN = 0.5
TIME_STEP = 0.2
PEAK_PRESSURE = 1.5
RADIUS_SQUARED = 36.0

MESH = pl.DeviceIdType.MESH
F32 = jnp.float32
BF16 = jnp.bfloat16

ORDERS = (("x", "y", "z"), ("y", "z", "x"), ("z", "x", "y"))
CHUNKS = ((0, 4, 0), (4, 3, 1), (7, 3, 2), (10, 3, 0), (13, 3, 1), (16, 3, 2))
WAVES = ((0, 1, 2), (3, 4, 5))
SPOTS = 36
NODES = 27


def iota(shape, dim):
    return lax.broadcasted_iota(jnp.int32, shape, dim)


def kernel(
    old, sends, asks_in, w, vel_in, mass_in, spot_x_in, spot_y_in,
    st, vout, *scratch,
):
    hbuf, sbuf, ubuf, gbuf = (scratch[n * 6:n * 6 + 6] for n in range(4))
    (
        sbuf_in, spread, psel, qsel, xs, wv, rem,
        vext, vcol, dtm, dtmc, press, pressc, ddx, ddy, dsm, s6, fm, cl, cr,
        rowpack, rowin, colpack, colin, corin,
        row_up, row_dn, row_up_in, row_dn_in, cl_in, cr_in, diag_in,
        cr2, row2, cr2_in, row2_in, diag2_in,
        asks, vel, mass, spot_x, spot_y,
        p1_s, p1_r, ix_s, ix_r, p2_s, p2_r, p3_s, p3_r, loc1, locx, loc2, loc3, wsem,
        hs, hr, e1_s, e1_r, e2_s, e2_r, load,
    ) = scratch[24:]
    di = lax.axis_index("gx")
    dj = lax.axis_index("gy")
    here = {"z": di // 2, "c": di % 2, "y": dj // 4, "x": dj % 4}

    def device(**moved):
        at = dict(here)
        for axis, step in moved.items():
            size = 2 if axis == "c" else 4
            at[axis] = (at[axis] + step) % size
        return (at["z"] * 2 + at["c"], at["y"] * 4 + at["x"])

    def plate(a, b):
        return ((di + a + 8) % 8, (dj + b + 16) % 16)

    around = [(a, b) for a in (-1, 0, 1) for b in (-1, 0, 1) if (a, b) != (0, 0)]
    partners = [device(**{axis: d, "c": c}) for axis in "xyz" for d in (1, 2, 3) for c in (0, 1)]
    partners.append(device(c=1))
    partners += [plate(a, b) for a, b in around]
    barrier = pltpu.get_barrier_semaphore()
    for partner in partners:
        pl.semaphore_signal(barrier, inc=1, device_id=partner, device_id_type=MESH)

    def remote(src, dst, ssem, rsem, target):
        return pltpu.make_async_remote_copy(
            src_ref=src, dst_ref=dst, send_sem=ssem, recv_sem=rsem, device_id=target, device_id_type=MESH
        )

    local1 = []
    for q, (first, count, order) in enumerate(CHUNKS):
        local1.append(
            pltpu.make_async_copy(old.at[pl.ds(first, count)], hbuf[q].at[here[ORDERS[order][0]]], loc1.at[q])
        )
        local1[q].start()
    localx = []
    for o, (ga, pa, qa) in enumerate(ORDERS):
        localx.append(pltpu.make_async_copy(sends, sbuf_in.at[o, here[ga]], locx.at[o]))
        localx[o].start()
    pairs = ((vel_in, vel), (mass_in, mass), (asks_in, asks), (spot_x_in, spot_x), (spot_y_in, spot_y))
    loads = [pltpu.make_async_copy(src, dst, load.at[n]) for n, (src, dst) in enumerate(pairs)]
    for copy in loads:
        copy.start()
    pl.semaphore_wait(barrier, len(partners))

    phase1 = {}

    def start_phase1(wave):
        for q in wave:
            first, count, order = CHUNKS[q]
            ga = ORDERS[order][0]
            phase1[q] = [
                remote(
                    old.at[pl.ds(first, count)], hbuf[q].at[here[ga]], p1_s.at[q, d - 1], p1_r.at[q, d - 1], device(**{ga: d})
                )
                for d in (1, 2, 3)
            ]
        for d in (0, 1, 2):
            for q in wave:
                phase1[q][d].start()

    lists = []
    for d in (1, 2, 3):
        for o, (ga, pa, qa) in enumerate(ORDERS):
            lists.append((o, remote(
                sends, sbuf_in.at[o, here[ga]], ix_s.at[o, d - 1], ix_r.at[o, d - 1], device(**{ga: d})
            )))
            lists[-1][1].start()
    start_phase1(WAVES[0])

    weights = [
        pltpu.make_async_copy(w.at[pl.ds(n * 32, 32)], wv.at[pl.ds(n * 32, 32)], wsem.at[n]) for n in range(4)
    ]
    for copy in weights:
        copy.start()

    for copy in loads:
        copy.wait()

    lane16 = iota((16, 128), 1)
    packed = jnp.zeros((16, 128), F32)
    for n in range(NODES):
        plane = vel[n]
        rowpack[n:n + 1, :] = plane[0:1, :]
        moved = plane if n == 0 else pltpu.roll(plane, n, 1)
        packed = jnp.where(lane16 == n, moved, packed)
        heavy = pltpu.roll(mass[n % 9], n + 32, 1)
        packed = jnp.where(lane16 == n + 32, heavy, packed)
    colpack[...] = packed
    for n in range(9):
        rowpack[32 + n:33 + n, :] = mass[n, 0:1, :]
    halo = (
        remote(rowpack, rowin, hs.at[0], hr.at[0], plate(-1, 0)),
        remote(colpack, colin, hs.at[1], hr.at[1], plate(0, -1)),
        remote(colpack.at[pl.ds(0, 8)], corin, hs.at[2], hr.at[2], plate(-1, -1)),
    )
    for copy in halo:
        copy.start()

    t192, c768 = iota((192, 128), 0), iota((192, 128), 1)
    aim, part = t192 // 6, t192 % 6
    on_p, on_q, on_c = aim // 8, (aim // 2) % 4, aim % 2
    for o, (ga, pa, qa) in enumerate(ORDERS):
        at = {ga: here[ga], pa: on_p, qa: on_q}
        stands = (((at["z"] * 2 + on_c) * 4 + at["y"]) * 4 + at["x"]) * 6 + part
        for m in range(6):
            spread[o, :, m * 128:(m + 1) * 128] = jnp.where(stands == c768 + m * 128, 1.0, 0.0).astype(BF16)
    r768 = iota((768, 256), 0)
    widen = jnp.where((r768 // 24) * 6 + r768 % 6 == iota((768, 256), 1), 1.0, 0.0).astype(BF16)
    source_of = (iota((768, 128), 0) // 6) % 4
    lanes768 = iota((768, 128), 1).astype(F32)

    phase2 = {}

    def selection(o):
        localx[o].wait()
        for of, copy in lists:
            if of == o:
                copy.wait_recv()
        table = jnp.concatenate(
            [sbuf_in[o, n].astype(F32) for n in range(4)] + [jnp.zeros((4, 768), F32)], axis=0
        ).astype(BF16)
        short = lax.dot_general(spread[o], table, (((1,), (1,)), ((), ())), preferred_element_type=F32)
        short = jnp.concatenate([short, jnp.zeros((64, 8), F32)], axis=0).astype(BF16)
        codes = jnp.dot(widen, short, preferred_element_type=F32)
        for sg in range(4):
            hit = (codes[:, sg:sg + 1] == lanes768) & (source_of == sg)
            psel[o, :, sg * 128:(sg + 1) * 128] = jnp.where(hit, 1.0, 0.0).astype(BF16)

    def arrived(q):
        local1[q].wait()
        for copy in phase1[q]:
            copy.wait_recv()

    def start_phase2(q):
        first, count, o = CHUNKS[q]
        ga, pa, qa = ORDERS[o]
        blocks = jnp.concatenate([hbuf[q][:, n].reshape(512, 128) for n in range(count)], axis=1)
        for half in range(2):
            rows = jnp.dot(psel[o, half * 384:(half + 1) * 384, :], blocks, preferred_element_type=F32)
            for t in range(16):
                sbuf[q][half * 2 + t // 8, t % 8] = rows[t * 24:(t + 1) * 24].astype(BF16)
        mine = here[pa]
        own = pltpu.make_async_copy(sbuf[q].at[mine], ubuf[q].at[mine], loc2.at[q])
        own.start()
        copies = [
            remote(sbuf[q].at[(mine + d) % 4], ubuf[q].at[mine], p2_s.at[q, d - 1], p2_r.at[q, d - 1], device(**{pa: d}))
            for d in (2, 1, 3)
        ]
        for copy in copies:
            copy.start()
        phase2[q] = (own, copies)

    phase3 = {}

    def start_phase3(q):
        first, count, o = CHUNKS[q]
        ga, pa, qa = ORDERS[o]
        own, copies = phase2[q]
        own.wait()
        for copy in copies:
            copy.wait_recv()
        mine = here[qa] * 2 + here["c"]
        own = pltpu.make_async_copy(ubuf[q].at[:, mine], gbuf[q].at[mine], loc3.at[q])
        own.start()
        copies = []
        for d in (2, 1, 3, 0):
            for c in (0, 1):
                if (d, c) != (0, 0):
                    there = ((here[qa] + d) % 4) * 2 + (here["c"] + c) % 2
                    slot = d * 2 + c - 1
                    copies.append(remote(
                        ubuf[q].at[:, there], gbuf[q].at[mine], p3_s.at[q, slot], p3_r.at[q, slot], device(**{qa: d, "c": c})
                    ))
        for copy in copies:
            copy.start()
        phase3[q] = (own, copies)

    def turn(first, last):
        def tile(g, carry):
            for k in range(3):
                wv[g, k] = wv[g, k].T
            return carry

        lax.fori_loop(first, last, tile, 0, unroll=4)

    def arrive(q):
        first, count, o = CHUNKS[q]
        own, copies = phase3[q]
        own.wait()
        for copy in copies:
            copy.wait_recv()
        rows = gbuf[q][...].astype(F32).reshape(768, count * 128).astype(BF16)
        picked = jnp.dot(qsel[o], rows, preferred_element_type=F32)
        for n in range(count):
            xs[pl.ds(first + n, 384, stride=24), :] = picked[:, n * 128:(n + 1) * 128]

    for o in range(3):
        selection(o)
    for q in WAVES[0]:
        arrived(q)
    start_phase1(WAVES[1])
    for q in WAVES[0]:
        start_phase2(q)

    asked = asks[...]
    origin = (asked * 10923) >> 16
    slot = asked - origin * 6
    place = {"z": origin >> 5, "c": (origin >> 4) & 1, "y": (origin >> 2) & 3, "x": origin & 3}
    wanted = [
        (((place[qa] * 2 + place["c"]) * 4 + place[pa]) * 24 + place[ga] * 6 + slot).astype(F32) for ga, pa, qa in ORDERS
    ]
    ridx_t = jnp.transpose(jnp.concatenate(wanted + [jnp.zeros((119, 128), F32)], axis=0))
    for q in range(3):
        for k in range(3):
            column = ridx_t[:, q * 3 + k:q * 3 + k + 1]
            for m in range(6):
                hit = column == (iota((128, 128), 1) + m * 128).astype(F32)
                qsel[q, k * 128:(k + 1) * 128, m * 128:(m + 1) * 128] = jnp.where(hit, 1.0, 0.0).astype(BF16)

    row24 = iota((24, 128), 0)
    lane24 = iota((24, 128), 1)
    node_x = (di * 16 + row24).astype(F32)
    node_y = (dj * 128 + lane24).astype(F32)
    next_y = (dj * 128 + 128).astype(F32)

    def spot(n, sums):
        main, side = sums
        sx = spot_x[n].astype(F32)
        sy = spot_y[n].astype(F32)
        far_x = (node_x - sx) ** 2
        main = main + jnp.exp(-(far_x + (node_y - sy) ** 2) / RADIUS_SQUARED)
        side = side + jnp.exp(-(far_x + (next_y - sy) ** 2) / RADIUS_SQUARED)
        return (main, side)

    main, side = lax.fori_loop(0, SPOTS, spot, (jnp.zeros((24, 128), F32), jnp.zeros((24, 128), F32)))
    press[...] = -PEAK_PRESSURE * main
    pressc[...] = jnp.where(lane24 == NODES - 1, -PEAK_PRESSURE * side, 0.0)

    for q in WAVES[1]:
        arrived(q)
        start_phase2(q)
    for copy in weights:
        copy.wait()
    for q in WAVES[0]:
        start_phase3(q)
    turn(0, 64)
    for q in WAVES[1]:
        start_phase3(q)

    for copy in halo:
        copy.wait_recv()
    low_i, high_i = (di > 0).astype(F32), (di < 7).astype(F32)
    low_j, high_j = (dj > 0).astype(F32), (dj < 15).astype(F32)
    first8 = iota((8, 128), 0) == 0
    row_mask = jnp.where(row24 < 16, 1.0, high_i)
    for n in range(NODES):
        vext[n, 0:16, :] = vel[n]
        vext[n, 16:24, :] = jnp.where(first8, rowin[n:n + 1, :] * high_i, 0.0)
    for n in range(9):
        dtm[n, 0:16, :] = TIME_STEP / mass[n]
        dtm[n, 16:24, :] = jnp.where(first8, high_i * TIME_STEP / rowin[32 + n:33 + n, :], 0.0)
    column = jnp.concatenate([colin[...], jnp.where(first8, corin[...] * high_i, 0.0)], axis=0)
    vcol[...] = jnp.where(lane24 < NODES, column * high_j, 0.0)
    heavy = pltpu.roll(jnp.concatenate([colin[...], corin[...]], axis=0), 96, 1)
    used = (lane24 < NODES) & (row24 < 17)
    dtmc[...] = jnp.where(used, high_j * row_mask * TIME_STEP / jnp.where(used, heavy, 1.0), 0.0)

    def differences():
        edge = lane24 == 127
        for n in range(NODES):
            v = vext[n]
            right = jnp.where(edge, vcol[:, n:n + 1], pltpu.roll(v, 127, 1))
            total = v + right
            delta = right - v
            total_up = pltpu.roll(total, 23, 0)
            delta_up = pltpu.roll(delta, 23, 0)
            ddx[n] = (total_up - total)[0:16]
            ddy[n] = (delta_up + delta)[0:16]
            dsm[n] = (total_up + total)[0:16]

    differences()
    for comp in range(6):
        s6[comp, 0] = jnp.zeros((16, 128), F32)
        s6[comp, 9] = jnp.zeros((16, 128), F32)

    turn(64, 128)
    for wave in WAVES:
        for q in wave:
            arrive(q)

    def block(g, carry):
        parts = [xs[pl.ds(pl.multiple_of((k * 128 + g) * 24, 8), 24), :] for k in range(3)]
        rem[pl.ds(pl.multiple_of(g * 24, 8), 24), :] = jnp.dot(
            jnp.concatenate(parts, axis=1).astype(BF16), wv[g].reshape(384, 128), preferred_element_type=F32
        )
        return carry

    lax.fori_loop(0, 128, block, 0, unroll=8)

    def elements(step):
        def layer(z, carry):
            def state(n):
                if step == 0:
                    return rem[pl.ds(z * 384 + n, 16, stride=24), :]
                return st[n, z]

            gx = [0.25 * (ddx[n * 9 + z] + ddx[n * 9 + z + 1]) for n in range(3)]
            gy = [0.25 * (ddy[n * 9 + z] + ddy[n * 9 + z + 1]) for n in range(3)]
            gz = [0.25 * (dsm[n * 9 + z + 1] - dsm[n * 9 + z]) for n in range(3)]
            strain = [
                TIME_STEP * gx[0],
                TIME_STEP * gy[1],
                TIME_STEP * gz[2],
                TIME_STEP * 0.5 * (gy[0] + gx[1]),
                TIME_STEP * 0.5 * (gz[1] + gy[2]),
                TIME_STEP * 0.5 * (gx[2] + gz[0]),
            ]
            trace = strain[0] + strain[1] + strain[2]
            lame = BULK - 2.0 * SHEAR / 3.0
            trial = []
            for n in range(6):
                value = state(n) + 2.0 * SHEAR * strain[n]
                if n < 3:
                    value = value + lame * trace
                trial.append(value)
            mean = (trial[0] + trial[1] + trial[2]) * (1.0 / 3.0)
            back = [state(6 + n) for n in range(6)]
            xi = [(trial[n] - mean if n < 3 else trial[n]) - back[n] for n in range(6)]
            norm = xi[0] ** 2 + xi[1] ** 2 + xi[2] ** 2 + 2.0 * (xi[3] ** 2 + xi[4] ** 2 + xi[5] ** 2)
            equiv = jnp.sqrt(1.5 * norm)
            epbar = state(18)
            excess = jnp.maximum(equiv - (YIELD_STRESS + HARD_ISO * epbar), 0.0)
            dgamma = excess * (1.0 / (3.0 * SHEAR + HARD_ISO + HARD_KIN))
            factor = dgamma / jnp.maximum(equiv, YIELD_STRESS)
            for n in range(6):
                shift = factor * xi[n]
                stress = trial[n] - 3.0 * SHEAR * shift
                plastic = state(12 + n) + 1.5 * shift
                st[n, z] = stress
                s6[n, z + 1] = stress
                st[6 + n, z] = back[n] + HARD_KIN * shift
                st[12 + n, z] = plastic
            st[18, z] = epbar + dgamma
            return carry

        lax.fori_loop(0, 8, layer, 0)

    along = ((0, 3, 5), (3, 1, 4), (5, 4, 2))
    inner = lane16 > 0
    zeros8 = jnp.zeros((8, 128), F32)

    def forces(last):
        right0 = jnp.zeros((16, 128), F32)
        right1 = jnp.zeros((16, 128), F32)
        left = jnp.zeros((24, 128), F32)
        for i in range(3):
            for k in range(9):
                n = i * 9 + k
                ax = -0.25 * (s6[along[0][i], k + 1] + s6[along[0][i], k])
                ay = -0.25 * (s6[along[1][i], k + 1] + s6[along[1][i], k])
                az = -0.25 * (s6[along[2][i], k] - s6[along[2][i], k + 1])
                near, far = az - ax, az + ax
                near_up, far_up = near + ay, far + ay
                roll0, roll1 = pltpu.roll(near_up, 1, 1), pltpu.roll(far_up, 1, 1)
                e0 = near - ay + jnp.where(inner, roll0, 0.0)
                e1 = far - ay + jnp.where(inner, roll1, 0.0)
                turn0 = roll0 if n == 0 else pltpu.roll(near_up, n + 1, 1)
                turn1 = roll1 if n == 0 else pltpu.roll(far_up, n + 1, 1)
                right0 = jnp.where(lane16 == n, turn0, right0)
                right1 = jnp.where(lane16 == n, turn1, right1)
                whole = jnp.concatenate([e0, zeros8], axis=0) + pltpu.roll(jnp.concatenate([e1, zeros8], axis=0), 1, 0)
                fm[n] = whole
                if last:
                    row2[n:n + 1, :] = whole[16:17]
                else:
                    row_up[n:n + 1, :] = whole[16:17]
                    row_dn[n:n + 1, :] = whole[0:1]
                    left = jnp.where(lane24 == n, whole if n == 0 else pltpu.roll(whole, n, 1), left)
        right = jnp.concatenate([right0, zeros8], axis=0) + pltpu.roll(jnp.concatenate([right1, zeros8], axis=0), 1, 0)
        return left, right

    elements(0)
    left, right = forces(False)
    cl[...] = left
    cr[...] = right
    row_up[32:40, :] = right[16:24]
    row_dn[32:40, :] = right[0:8]
    low, high = pl.ds(0, 8), pl.ds(16, 8)
    round1 = (
        remote(row_up, row_up_in, e1_s.at[0], e1_r.at[0], plate(1, 0)),
        remote(row_dn, row_dn_in, e1_s.at[1], e1_r.at[1], plate(-1, 0)),
        remote(cr, cr_in, e1_s.at[2], e1_r.at[2], plate(0, 1)),
        remote(cl, cl_in, e1_s.at[3], e1_r.at[3], plate(0, -1)),
        remote(cr.at[high], diag_in.at[0], e1_s.at[4], e1_r.at[4], plate(1, 1)),
        remote(cr.at[low], diag_in.at[1], e1_s.at[5], e1_r.at[5], plate(-1, 1)),
        remote(cl.at[high], diag_in.at[2], e1_s.at[6], e1_r.at[6], plate(1, -1)),
        remote(cl.at[low], diag_in.at[3], e1_s.at[7], e1_r.at[7], plate(-1, -1)),
    )
    for copy in round1:
        copy.start()
    for copy in round1:
        copy.wait_recv()

    def ends(at_low, at_high):
        return jnp.concatenate([
            jnp.where(first8, at_low * low_i, 0.0), zeros8, jnp.where(first8, at_high * high_i, 0.0)
        ], axis=0)

    add_left = low_j * (cr_in[...] + ends(diag_in[0], diag_in[1]))
    add_right = high_j * (cl_in[...] + ends(diag_in[2], diag_in[3]))
    col_force = cr[...] + add_right + ends(row_up_in[32:40], row_dn_in[32:40]) + pressc[...]
    vcol[...] = vcol[...] + col_force * dtmc[...]
    for n in range(NODES):
        rows = jnp.concatenate([
            jnp.where(first8, row_up_in[n:n + 1] * low_i, 0.0), zeros8, jnp.where(first8, row_dn_in[n:n + 1] * high_i, 0.0)
        ], axis=0)
        force = fm[n] + rows + jnp.where(lane24 == 0, add_left[:, n:n + 1], 0.0)
        if n == NODES - 1:
            force = force + press[...]
        vext[n] = vext[n] + force * dtm[n % 9]

    differences()
    elements(1)
    left, right = forces(True)
    cr2[...] = right
    round2 = (
        remote(row2, row2_in, e2_s.at[0], e2_r.at[0], plate(1, 0)),
        remote(cr2, cr2_in, e2_s.at[1], e2_r.at[1], plate(0, 1)),
        remote(cr2.at[high], diag2_in, e2_s.at[2], e2_r.at[2], plate(1, 1)),
    )
    for copy in round2:
        copy.start()
    for copy in round2:
        copy.wait_recv()
    corner = jnp.concatenate([jnp.where(first8, diag2_in[...] * low_i, 0.0), zeros8], axis=0)
    add_left = low_j * (cr2_in[0:16] + corner)
    for n in range(NODES):
        rows = jnp.concatenate([jnp.where(first8, row2_in[n:n + 1] * low_i, 0.0), zeros8], axis=0)
        force = fm[n, 0:16] + rows + jnp.where(lane16 == 0, add_left[:, n:n + 1], 0.0)
        if n == NODES - 1:
            force = force + press[0:16]
        vout[n] = vext[n, 0:16] + force * dtm[n % 9, 0:16]

    for o, copy in lists:
        copy.wait_send()
    for q in range(6):
        for copy in phase1[q] + phase2[q][1] + phase3[q][1]:
            copy.wait_send()
    for copy in halo + round1 + round2:
        copy.wait_send()


def body(
    old_state,
    send_block,
    receive_slot_table,
    interpolation_weight_tiles,
    velocity,
    node_mass,
    spot_x,
    spot_y,
):
    vmem = pl.BlockSpec(memory_space=pltpu.VMEM)
    hbm = pl.BlockSpec(memory_space=pltpu.HBM)
    counts = [chunk[1] for chunk in CHUNKS]
    scratch = (
        [pltpu.VMEM((4, n, 128, 128), BF16) for n in counts]
        + [pltpu.VMEM((4, 8, 24, n * 128), BF16) for n in counts]
        + [pltpu.VMEM((4, 8, 24, n * 128), BF16) for n in counts]
        + [pltpu.VMEM((8, 4, 24, n * 128), BF16) for n in counts]
        + [
            pltpu.VMEM((3, 4, 1, 768), jnp.int32),
            pltpu.VMEM((3, 192, 768), BF16),
            pltpu.VMEM((3, 768, 512), BF16),
            pltpu.VMEM((3, 384, 768), BF16),
            pltpu.VMEM((384 * 24, 128), F32),
            pltpu.VMEM((128, 3, 128, 128), BF16),
            pltpu.VMEM((128 * 24, 128), F32),
            pltpu.VMEM((27, 24, 128), F32),
            pltpu.VMEM((24, 128), F32),
            pltpu.VMEM((9, 24, 128), F32),
            pltpu.VMEM((24, 128), F32),
            pltpu.VMEM((24, 128), F32),
            pltpu.VMEM((24, 128), F32),
            pltpu.VMEM((27, 16, 128), F32),
            pltpu.VMEM((27, 16, 128), F32),
            pltpu.VMEM((27, 16, 128), F32),
            pltpu.VMEM((6, 10, 16, 128), F32),
            pltpu.VMEM((27, 24, 128), F32),
            pltpu.VMEM((24, 128), F32),
            pltpu.VMEM((24, 128), F32),
            pltpu.VMEM((48, 128), F32),
            pltpu.VMEM((48, 128), F32),
            pltpu.VMEM((16, 128), F32),
            pltpu.VMEM((16, 128), F32),
            pltpu.VMEM((8, 128), F32),
            pltpu.VMEM((40, 128), F32),
            pltpu.VMEM((40, 128), F32),
            pltpu.VMEM((40, 128), F32),
            pltpu.VMEM((40, 128), F32),
            pltpu.VMEM((24, 128), F32),
            pltpu.VMEM((24, 128), F32),
            pltpu.VMEM((4, 8, 128), F32),
            pltpu.VMEM((24, 128), F32),
            pltpu.VMEM((32, 128), F32),
            pltpu.VMEM((24, 128), F32),
            pltpu.VMEM((32, 128), F32),
            pltpu.VMEM((8, 128), F32),
            pltpu.VMEM((3, 128), jnp.int32),
            pltpu.VMEM((27, 16, 128), F32),
            pltpu.VMEM((9, 16, 128), F32),
            pltpu.SMEM((36,), jnp.int32),
            pltpu.SMEM((36,), jnp.int32),
        ]
        + [
            pltpu.SemaphoreType.DMA(shape)
            for shape in (
                (6, 3), (6, 3), (3, 3), (3, 3), (6, 3), (6, 3), (6, 7), (6, 7), (6,), (3,), (6,), (6,), (4,),
                (3,), (3,), (8,), (8,), (3,), (3,), (5,),
            )
        ]
    )
    state, moved = pl.pallas_call(
        kernel,
        out_shape=(
            jax.ShapeDtypeStruct((19, 8, 16, 128), F32),
            jax.ShapeDtypeStruct((27, 16, 128), F32),
        ),
        in_specs=[hbm] * 8,
        out_specs=(vmem, vmem),
        scratch_shapes=scratch,
        compiler_params=pltpu.CompilerParams(
            collective_id=0, has_side_effects=True, vmem_limit_bytes=48 * 2**20
        ),
        name="remap_and_steps",
    )(*(
        pltpu.with_memory_space_constraint(array, pltpu.HBM)
        for array in (
            old_state.transpose(1, 0, 2),
            send_block,
            receive_slot_table.T,
            interpolation_weight_tiles,
            velocity.reshape(27, 16, 128),
            node_mass,
            spot_x,
            spot_y,
        )
    ))
    return (state, moved.reshape(3, 9, 16, 128))


def solution(mesh):
    return jax.shard_map(
        body,
        mesh=mesh,
        in_specs=(
            P(("gx", "gy"), None, None),
            P(("gx", "gy"), None),
            P(("gx", "gy"), None),
            P(("gx", "gy"), None, None, None),
            P(None, None, "gx", "gy"),
            P(None, "gx", "gy"),
            P(),
            P(),
        ),
        out_specs=(P(None, None, "gx", "gy"), P(None, None, "gx", "gy")),
        check_vma=False,
    )
```

```python
import jax
import jax.numpy as jnp
from jax import lax
from jax.experimental import pallas as pl
from jax.experimental.pallas import tpu as pltpu
from jax.sharding import PartitionSpec as P

SHEAR = 1.0
BULK = 2.0
YIELD_STRESS = 2.0
HARD_ISO = 0.3
HARD_KIN = 0.5
TIME_STEP = 0.2
PEAK_PRESSURE = 1.5
RADIUS_SQUARED = 36.0

MESH = pl.DeviceIdType.MESH
F32 = jnp.float32
BF16 = jnp.bfloat16

ORDERS = (("x", "y", "z"), ("y", "z", "x"), ("z", "x", "y"))
CHUNKS = ((0, 4, 0), (4, 3, 1), (7, 3, 2), (10, 3, 0), (13, 3, 1), (16, 3, 2))
WAVES = ((0, 1, 2), (3, 4, 5))
SPOTS = 36
NODES = 27


def iota(shape, dim):
    return lax.broadcasted_iota(jnp.int32, shape, dim)


def kernel(
    old, sends, asks_in, w, vel_in, mass_in, spot_x_in, spot_y_in,
    state_out, v_out, *scratch,
):
    hbuf, sbuf, ubuf, gbuf = (scratch[n * 6:n * 6 + 6] for n in range(4))
    (
        sbuf_in, spread, psel, qsel, xs, wv, rem,
        vext, vcol, dtm, dtmc, press, pressc, ddx, ddy, dsm, s6, fm, cl, cr,
        rowpack, rowin, colpack, colin, corin,
        row_up, row_dn, row_up_in, row_dn_in, cl_in, cr_in, diag_in,
        cr2, row2, cr2_in, row2_in, diag2_in,
        asks, vel, mass, spot_x, spot_y, st, vout,
        p1_s, p1_r, ix_s, ix_r, p2_s, p2_r, p3_s, p3_r, loc1, locx, loc2, loc3, wsem,
        hs, hr, e1_s, e1_r, e2_s, e2_r, load, out_sem,
    ) = scratch[24:]
    di = lax.axis_index("gx")
    dj = lax.axis_index("gy")
    here = {"z": di // 2, "c": di % 2, "y": dj // 4, "x": dj % 4}

    def device(**moved):
        at = dict(here)
        for axis, step in moved.items():
            size = 2 if axis == "c" else 4
            at[axis] = (at[axis] + step) % size
        return (at["z"] * 2 + at["c"], at["y"] * 4 + at["x"])

    def plate(a, b):
        return ((di + a + 8) % 8, (dj + b + 16) % 16)

    around = [(a, b) for a in (-1, 0, 1) for b in (-1, 0, 1) if (a, b) != (0, 0)]
    partners = [device(**{axis: d, "c": c}) for axis in "xyz" for d in (1, 2, 3) for c in (0, 1)]
    partners.append(device(c=1))
    partners += [plate(a, b) for a, b in around if b != 0]
    barrier = pltpu.get_barrier_semaphore()
    for partner in partners:
        pl.semaphore_signal(barrier, inc=1, device_id=partner, device_id_type=MESH)

    def remote(src, dst, ssem, rsem, target):
        return pltpu.make_async_remote_copy(
            src_ref=src, dst_ref=dst, send_sem=ssem, recv_sem=rsem, device_id=target, device_id_type=MESH
        )

    local1 = []
    for q, (first, count, order) in enumerate(CHUNKS):
        local1.append(
            pltpu.make_async_copy(old.at[pl.ds(first, count)], hbuf[q].at[here[ORDERS[order][0]]], loc1.at[q])
        )
        local1[q].start()
    localx = []
    for o, (ga, pa, qa) in enumerate(ORDERS):
        localx.append(pltpu.make_async_copy(sends, sbuf_in.at[o, here[ga]], locx.at[o]))
        localx[o].start()
    pairs = ((vel_in, vel), (mass_in, mass), (asks_in, asks), (spot_x_in, spot_x), (spot_y_in, spot_y))
    loads = [pltpu.make_async_copy(src, dst, load.at[n]) for n, (src, dst) in enumerate(pairs)]
    for copy in loads:
        copy.start()
    pl.semaphore_wait(barrier, len(partners))

    phase1, onward = {}, {}

    def start_phase1(wave):
        for q in wave:
            first, count, order = CHUNKS[q]
            ga = ORDERS[order][0]
            phase1[q] = [
                remote(
                    old.at[pl.ds(first, count)], hbuf[q].at[here[ga]], p1_s.at[q, n], p1_r.at[q, n], device(**{ga: d})
                )
                for n, d in enumerate((1, 3))
            ]
        for n in (0, 1):
            for q in wave:
                phase1[q][n].start()

    def start_onward(wave):
        for q in wave:
            first, count, order = CHUNKS[q]
            ga = ORDERS[order][0]
            half = count // 2 if q % 2 == 0 else count - count // 2
            onward[q] = []
            for n, (d, back, part) in enumerate(((1, 3, pl.ds(0, half)), (3, 1, pl.ds(half, count - half)))):
                phase1[q][n].wait_recv()
                held = hbuf[q].at[(here[ga] + back) % 4, part]
                onward[q].append(remote(held, held, p1_s.at[q, 2 + n], p1_r.at[q, 2 + n], device(**{ga: d})))
                onward[q][n].start()

    lists = []
    for d in (1, 2, 3):
        for o, (ga, pa, qa) in enumerate(ORDERS):
            lists.append((o, remote(
                sends, sbuf_in.at[o, here[ga]], ix_s.at[o, d - 1], ix_r.at[o, d - 1], device(**{ga: d})
            )))
            lists[-1][1].start()
    start_phase1(WAVES[0])
    start_phase1(WAVES[1])

    weights = [
        pltpu.make_async_copy(w.at[pl.ds(n * 32, 32)], wv.at[pl.ds(n * 32, 32)], wsem.at[n]) for n in range(4)
    ]
    for copy in weights:
        copy.start()

    for copy in loads:
        copy.wait()

    lane16 = iota((16, 128), 1)
    packed = jnp.zeros((16, 128), F32)
    for n in range(NODES):
        plane = vel[n]
        rowpack[n:n + 1, :] = plane[0:1, :]
        moved = plane if n == 0 else pltpu.roll(plane, n, 1)
        packed = jnp.where(lane16 == n, moved, packed)
        heavy = pltpu.roll(mass[n % 9], n + 32, 1)
        packed = jnp.where(lane16 == n + 32, heavy, packed)
    colpack[...] = packed
    for n in range(9):
        rowpack[32 + n:33 + n, :] = mass[n, 0:1, :]
    halo = (
        remote(rowpack, rowin, hs.at[0], hr.at[0], plate(-1, 0)),
        remote(colpack, colin, hs.at[1], hr.at[1], plate(0, -1)),
        remote(colpack.at[pl.ds(0, 8)], corin, hs.at[2], hr.at[2], plate(-1, -1)),
    )
    for copy in halo:
        copy.start()

    t192, c768 = iota((192, 128), 0), iota((192, 128), 1)
    aim, part = t192 // 6, t192 % 6
    on_p, on_q, on_c = aim // 8, (aim // 2) % 4, aim % 2
    for o, (ga, pa, qa) in enumerate(ORDERS):
        at = {ga: here[ga], pa: on_p, qa: on_q}
        stands = (((at["z"] * 2 + on_c) * 4 + at["y"]) * 4 + at["x"]) * 6 + part
        for m in range(6):
            spread[o, :, m * 128:(m + 1) * 128] = jnp.where(stands == c768 + m * 128, 1.0, 0.0).astype(BF16)
    r768 = iota((768, 256), 0)
    widen = jnp.where((r768 // 24) * 6 + r768 % 6 == iota((768, 256), 1), 1.0, 0.0).astype(BF16)
    source_of = (iota((768, 128), 0) // 6) % 4
    lanes768 = iota((768, 128), 1).astype(F32)

    phase2 = {}

    def selection(o):
        localx[o].wait()
        for of, copy in lists:
            if of == o:
                copy.wait_recv()
        table = jnp.concatenate(
            [sbuf_in[o, n].astype(F32) for n in range(4)] + [jnp.zeros((4, 768), F32)], axis=0
        ).astype(BF16)
        short = lax.dot_general(spread[o], table, (((1,), (1,)), ((), ())), preferred_element_type=F32)
        short = jnp.concatenate([short, jnp.zeros((64, 8), F32)], axis=0).astype(BF16)
        codes = jnp.dot(widen, short, preferred_element_type=F32)
        for sg in range(4):
            hit = (codes[:, sg:sg + 1] == lanes768) & (source_of == sg)
            psel[o, :, sg * 128:(sg + 1) * 128] = jnp.where(hit, 1.0, 0.0).astype(BF16)

    def arrived(q):
        local1[q].wait()
        for copy in onward[q]:
            copy.wait_recv()

    def start_phase2(q):
        first, count, o = CHUNKS[q]
        ga, pa, qa = ORDERS[o]
        blocks = jnp.concatenate([hbuf[q][:, n].reshape(512, 128) for n in range(count)], axis=1)
        for half in range(2):
            rows = jnp.dot(psel[o, half * 384:(half + 1) * 384, :], blocks, preferred_element_type=F32)
            for t in range(16):
                sbuf[q][half * 2 + t // 8, t % 8] = rows[t * 24:(t + 1) * 24].astype(BF16)
        mine = here[pa]
        own = pltpu.make_async_copy(sbuf[q].at[mine], ubuf[q].at[mine], loc2.at[q])
        own.start()
        copies = [
            remote(sbuf[q].at[(mine + d) % 4], ubuf[q].at[mine], p2_s.at[q, d - 1], p2_r.at[q, d - 1], device(**{pa: d}))
            for d in (2, 1, 3)
        ]
        for copy in copies:
            copy.start()
        phase2[q] = (own, copies)

    phase3 = {}

    def start_phase3(q):
        first, count, o = CHUNKS[q]
        ga, pa, qa = ORDERS[o]
        own, copies = phase2[q]
        own.wait()
        for copy in copies:
            copy.wait_recv()
        mine = here[qa] * 2 + here["c"]
        own = pltpu.make_async_copy(ubuf[q].at[:, mine], gbuf[q].at[mine], loc3.at[q])
        own.start()
        copies = []
        for d in (2, 1, 3, 0):
            for c in (0, 1):
                if (d, c) != (0, 0):
                    there = ((here[qa] + d) % 4) * 2 + (here["c"] + c) % 2
                    slot = d * 2 + c - 1
                    copies.append(remote(
                        ubuf[q].at[:, there], gbuf[q].at[mine], p3_s.at[q, slot], p3_r.at[q, slot], device(**{qa: d, "c": c})
                    ))
        for copy in copies:
            copy.start()
        phase3[q] = (own, copies)

    def turn(first, last):
        def tile(g, carry):
            for k in range(3):
                wv[g, k] = wv[g, k].T
            return carry

        lax.fori_loop(first, last, tile, 0, unroll=4)

    def arrive(q):
        first, count, o = CHUNKS[q]
        own, copies = phase3[q]
        own.wait()
        for copy in copies:
            copy.wait_recv()
        rows = gbuf[q][...].astype(F32).reshape(768, count * 128).astype(BF16)
        picked = jnp.dot(qsel[o], rows, preferred_element_type=F32)
        for n in range(count):
            xs[pl.ds(first + n, 384, stride=24), :] = picked[:, n * 128:(n + 1) * 128]

    selection(0)
    start_onward(WAVES[0])
    selection(1)
    selection(2)
    start_onward(WAVES[1])
    for q in WAVES[0]:
        arrived(q)
        start_phase2(q)

    asked = asks[...]
    origin = (asked * 10923) >> 16
    slot = asked - origin * 6
    place = {"z": origin >> 5, "c": (origin >> 4) & 1, "y": (origin >> 2) & 3, "x": origin & 3}
    wanted = [
        (((place[qa] * 2 + place["c"]) * 4 + place[pa]) * 24 + place[ga] * 6 + slot).astype(F32) for ga, pa, qa in ORDERS
    ]
    ridx_t = jnp.transpose(jnp.concatenate(wanted + [jnp.zeros((119, 128), F32)], axis=0))
    for q in range(3):
        for k in range(3):
            column = ridx_t[:, q * 3 + k:q * 3 + k + 1]
            for m in range(6):
                hit = column == (iota((128, 128), 1) + m * 128).astype(F32)
                qsel[q, k * 128:(k + 1) * 128, m * 128:(m + 1) * 128] = jnp.where(hit, 1.0, 0.0).astype(BF16)

    row24 = iota((24, 128), 0)
    lane24 = iota((24, 128), 1)
    node_x = (di * 16 + row24).astype(F32)
    node_y = (dj * 128 + lane24).astype(F32)
    next_y = (dj * 128 + 128).astype(F32)

    def spot(n, sums):
        main, side = sums
        sx = spot_x[n].astype(F32)
        sy = spot_y[n].astype(F32)
        far_x = (node_x - sx) ** 2
        main = main + jnp.exp(-(far_x + (node_y - sy) ** 2) / RADIUS_SQUARED)
        side = side + jnp.exp(-(far_x + (next_y - sy) ** 2) / RADIUS_SQUARED)
        return (main, side)

    main, side = lax.fori_loop(0, SPOTS, spot, (jnp.zeros((24, 128), F32), jnp.zeros((24, 128), F32)))
    press[...] = -PEAK_PRESSURE * main
    pressc[...] = jnp.where(lane24 == NODES - 1, -PEAK_PRESSURE * side, 0.0)

    for q in WAVES[1]:
        arrived(q)
        start_phase2(q)
    for copy in weights:
        copy.wait()
    for q in WAVES[0]:
        start_phase3(q)
    turn(0, 64)
    for q in WAVES[1]:
        start_phase3(q)

    for copy in halo:
        copy.wait_recv()
    low_i, high_i = (di > 0).astype(F32), (di < 7).astype(F32)
    low_j, high_j = (dj > 0).astype(F32), (dj < 15).astype(F32)
    first8 = iota((8, 128), 0) == 0
    row_mask = jnp.where(row24 < 16, 1.0, high_i)
    for n in range(NODES):
        vext[n, 0:16, :] = vel[n]
        vext[n, 16:24, :] = jnp.where(first8, rowin[n:n + 1, :] * high_i, 0.0)
    for n in range(9):
        dtm[n, 0:16, :] = TIME_STEP / mass[n]
        dtm[n, 16:24, :] = jnp.where(first8, high_i * TIME_STEP / rowin[32 + n:33 + n, :], 0.0)
    column = jnp.concatenate([colin[...], jnp.where(first8, corin[...] * high_i, 0.0)], axis=0)
    vcol[...] = jnp.where(lane24 < NODES, column * high_j, 0.0)
    heavy = pltpu.roll(jnp.concatenate([colin[...], corin[...]], axis=0), 96, 1)
    used = (lane24 < NODES) & (row24 < 17)
    dtmc[...] = jnp.where(used, high_j * row_mask * TIME_STEP / jnp.where(used, heavy, 1.0), 0.0)

    def differences():
        edge = lane24 == 127
        for n in range(NODES):
            v = vext[n]
            right = jnp.where(edge, vcol[:, n:n + 1], pltpu.roll(v, 127, 1))
            total = v + right
            delta = right - v
            total_up = pltpu.roll(total, 23, 0)
            delta_up = pltpu.roll(delta, 23, 0)
            ddx[n] = (total_up - total)[0:16]
            ddy[n] = (delta_up + delta)[0:16]
            dsm[n] = (total_up + total)[0:16]

    differences()
    for comp in range(6):
        s6[comp, 0] = jnp.zeros((16, 128), F32)
        s6[comp, 9] = jnp.zeros((16, 128), F32)

    turn(64, 128)
    for wave in WAVES:
        for q in wave:
            arrive(q)

    def block(g, carry):
        parts = [xs[pl.ds(pl.multiple_of((k * 128 + g) * 24, 8), 24), :] for k in range(3)]
        rem[pl.ds(pl.multiple_of(g * 24, 8), 24), :] = jnp.dot(
            jnp.concatenate(parts, axis=1).astype(BF16), wv[g].reshape(384, 128), preferred_element_type=F32
        )
        return carry

    lax.fori_loop(0, 128, block, 0, unroll=16)

    def elements(step):
        def layer(z, carry):
            def state(n):
                if step == 0:
                    return rem[pl.ds(z * 384 + n, 16, stride=24), :]
                return st[n, z]

            gx = [0.25 * (ddx[n * 9 + z] + ddx[n * 9 + z + 1]) for n in range(3)]
            gy = [0.25 * (ddy[n * 9 + z] + ddy[n * 9 + z + 1]) for n in range(3)]
            gz = [0.25 * (dsm[n * 9 + z + 1] - dsm[n * 9 + z]) for n in range(3)]
            strain = [
                TIME_STEP * gx[0],
                TIME_STEP * gy[1],
                TIME_STEP * gz[2],
                TIME_STEP * 0.5 * (gy[0] + gx[1]),
                TIME_STEP * 0.5 * (gz[1] + gy[2]),
                TIME_STEP * 0.5 * (gx[2] + gz[0]),
            ]
            trace = strain[0] + strain[1] + strain[2]
            lame = BULK - 2.0 * SHEAR / 3.0
            trial = []
            for n in range(6):
                value = state(n) + 2.0 * SHEAR * strain[n]
                if n < 3:
                    value = value + lame * trace
                trial.append(value)
            mean = (trial[0] + trial[1] + trial[2]) * (1.0 / 3.0)
            back = [state(6 + n) for n in range(6)]
            xi = [(trial[n] - mean if n < 3 else trial[n]) - back[n] for n in range(6)]
            norm = xi[0] ** 2 + xi[1] ** 2 + xi[2] ** 2 + 2.0 * (xi[3] ** 2 + xi[4] ** 2 + xi[5] ** 2)
            equiv = jnp.sqrt(1.5 * norm)
            epbar = state(18)
            excess = jnp.maximum(equiv - (YIELD_STRESS + HARD_ISO * epbar), 0.0)
            dgamma = excess * (1.0 / (3.0 * SHEAR + HARD_ISO + HARD_KIN))
            factor = dgamma / jnp.maximum(equiv, YIELD_STRESS)
            for n in range(6):
                shift = factor * xi[n]
                stress = trial[n] - 3.0 * SHEAR * shift
                plastic = state(12 + n) + 1.5 * shift
                st[n, z] = stress
                s6[n, z + 1] = stress
                st[6 + n, z] = back[n] + HARD_KIN * shift
                st[12 + n, z] = plastic
            st[18, z] = epbar + dgamma
            return carry

        lax.fori_loop(0, 8, layer, 0)

    along = ((0, 3, 5), (3, 1, 4), (5, 4, 2))
    inner = lane16 > 0
    zeros8 = jnp.zeros((8, 128), F32)

    def forces(last):
        right0 = jnp.zeros((16, 128), F32)
        right1 = jnp.zeros((16, 128), F32)
        left = jnp.zeros((24, 128), F32)
        for i in range(3):
            for k in range(9):
                n = i * 9 + k
                ax = -0.25 * (s6[along[0][i], k + 1] + s6[along[0][i], k])
                ay = -0.25 * (s6[along[1][i], k + 1] + s6[along[1][i], k])
                az = -0.25 * (s6[along[2][i], k] - s6[along[2][i], k + 1])
                near, far = az - ax, az + ax
                near_up, far_up = near + ay, far + ay
                roll0, roll1 = pltpu.roll(near_up, 1, 1), pltpu.roll(far_up, 1, 1)
                e0 = near - ay + jnp.where(inner, roll0, 0.0)
                e1 = far - ay + jnp.where(inner, roll1, 0.0)
                turn0 = roll0 if n == 0 else pltpu.roll(near_up, n + 1, 1)
                turn1 = roll1 if n == 0 else pltpu.roll(far_up, n + 1, 1)
                right0 = jnp.where(lane16 == n, turn0, right0)
                right1 = jnp.where(lane16 == n, turn1, right1)
                whole = jnp.concatenate([e0, zeros8], axis=0) + pltpu.roll(jnp.concatenate([e1, zeros8], axis=0), 1, 0)
                fm[n] = whole
                if last:
                    row2[n:n + 1, :] = whole[16:17]
                else:
                    row_up[n:n + 1, :] = whole[16:17]
                    row_dn[n:n + 1, :] = whole[0:1]
                    left = jnp.where(lane24 == n, whole if n == 0 else pltpu.roll(whole, n, 1), left)
        right = jnp.concatenate([right0, zeros8], axis=0) + pltpu.roll(jnp.concatenate([right1, zeros8], axis=0), 1, 0)
        return left, right

    elements(0)
    left, right = forces(False)
    cl[...] = left
    cr[...] = right
    row_up[32:40, :] = right[16:24]
    row_dn[32:40, :] = right[0:8]
    low, high = pl.ds(0, 8), pl.ds(16, 8)
    round1 = (
        remote(cr.at[high], diag_in.at[0], e1_s.at[4], e1_r.at[4], plate(1, 1)),
        remote(cr.at[low], diag_in.at[1], e1_s.at[5], e1_r.at[5], plate(-1, 1)),
        remote(cl.at[high], diag_in.at[2], e1_s.at[6], e1_r.at[6], plate(1, -1)),
        remote(cl.at[low], diag_in.at[3], e1_s.at[7], e1_r.at[7], plate(-1, -1)),
        remote(cr, cr_in, e1_s.at[2], e1_r.at[2], plate(0, 1)),
        remote(cl, cl_in, e1_s.at[3], e1_r.at[3], plate(0, -1)),
        remote(row_up, row_up_in, e1_s.at[0], e1_r.at[0], plate(1, 0)),
        remote(row_dn, row_dn_in, e1_s.at[1], e1_r.at[1], plate(-1, 0)),
    )
    for copy in round1:
        copy.start()
    for copy in round1:
        copy.wait_recv()

    def ends(at_low, at_high):
        return jnp.concatenate([
            jnp.where(first8, at_low * low_i, 0.0), zeros8, jnp.where(first8, at_high * high_i, 0.0)
        ], axis=0)

    add_left = low_j * (cr_in[...] + ends(diag_in[0], diag_in[1]))
    add_right = high_j * (cl_in[...] + ends(diag_in[2], diag_in[3]))
    col_force = cr[...] + add_right + ends(row_up_in[32:40], row_dn_in[32:40]) + pressc[...]
    vcol[...] = vcol[...] + col_force * dtmc[...]
    for n in range(NODES):
        rows = jnp.concatenate([
            jnp.where(first8, row_up_in[n:n + 1] * low_i, 0.0), zeros8, jnp.where(first8, row_dn_in[n:n + 1] * high_i, 0.0)
        ], axis=0)
        force = fm[n] + rows + jnp.where(lane24 == 0, add_left[:, n:n + 1], 0.0)
        if n == NODES - 1:
            force = force + press[...]
        vext[n] = vext[n] + force * dtm[n % 9]

    differences()
    elements(1)
    left, right = forces(True)
    cr2[...] = right
    round2 = (
        remote(cr2.at[high], diag2_in, e2_s.at[2], e2_r.at[2], plate(1, 1)),
        remote(cr2, cr2_in, e2_s.at[1], e2_r.at[1], plate(0, 1)),
        remote(row2, row2_in, e2_s.at[0], e2_r.at[0], plate(1, 0)),
    )
    for copy in round2:
        copy.start()
    state_copy = pltpu.make_async_copy(st, state_out, out_sem.at[0])
    state_copy.start()
    for copy in round2:
        copy.wait_recv()
    corner = jnp.concatenate([jnp.where(first8, diag2_in[...] * low_i, 0.0), zeros8], axis=0)
    add_left = low_j * (cr2_in[0:16] + corner)
    for n in range(NODES):
        rows = jnp.concatenate([jnp.where(first8, row2_in[n:n + 1] * low_i, 0.0), zeros8], axis=0)
        force = fm[n, 0:16] + rows + jnp.where(lane16 == 0, add_left[:, n:n + 1], 0.0)
        if n == NODES - 1:
            force = force + press[0:16]
        vout[n] = vext[n, 0:16] + force * dtm[n % 9, 0:16]

    v_copy = pltpu.make_async_copy(vout, v_out, out_sem.at[1])
    v_copy.start()
    for o, copy in lists:
        copy.wait_send()
    for q in range(6):
        for copy in phase1[q] + onward[q] + phase2[q][1] + phase3[q][1]:
            copy.wait_send()
    for copy in halo + round1 + round2:
        copy.wait_send()
    state_copy.wait()
    v_copy.wait()


def body(
    old_state,
    send_block,
    receive_slot_table,
    interpolation_weight_tiles,
    velocity,
    node_mass,
    spot_x,
    spot_y,
):
    anywhere = pl.BlockSpec(memory_space=pl.ANY)
    hbm = pl.BlockSpec(memory_space=pltpu.HBM)
    counts = [chunk[1] for chunk in CHUNKS]
    scratch = (
        [pltpu.VMEM((4, n, 128, 128), BF16) for n in counts]
        + [pltpu.VMEM((4, 8, 24, n * 128), BF16) for n in counts]
        + [pltpu.VMEM((4, 8, 24, n * 128), BF16) for n in counts]
        + [pltpu.VMEM((8, 4, 24, n * 128), BF16) for n in counts]
        + [
            pltpu.VMEM((3, 4, 1, 768), jnp.int32),
            pltpu.VMEM((3, 192, 768), BF16),
            pltpu.VMEM((3, 768, 512), BF16),
            pltpu.VMEM((3, 384, 768), BF16),
            pltpu.VMEM((384 * 24, 128), F32),
            pltpu.VMEM((128, 3, 128, 128), BF16),
            pltpu.VMEM((128 * 24, 128), F32),
            pltpu.VMEM((27, 24, 128), F32),
            pltpu.VMEM((24, 128), F32),
            pltpu.VMEM((9, 24, 128), F32),
            pltpu.VMEM((24, 128), F32),
            pltpu.VMEM((24, 128), F32),
            pltpu.VMEM((24, 128), F32),
            pltpu.VMEM((27, 16, 128), F32),
            pltpu.VMEM((27, 16, 128), F32),
            pltpu.VMEM((27, 16, 128), F32),
            pltpu.VMEM((6, 10, 16, 128), F32),
            pltpu.VMEM((27, 24, 128), F32),
            pltpu.VMEM((24, 128), F32),
            pltpu.VMEM((24, 128), F32),
            pltpu.VMEM((48, 128), F32),
            pltpu.VMEM((48, 128), F32),
            pltpu.VMEM((16, 128), F32),
            pltpu.VMEM((16, 128), F32),
            pltpu.VMEM((8, 128), F32),
            pltpu.VMEM((40, 128), F32),
            pltpu.VMEM((40, 128), F32),
            pltpu.VMEM((40, 128), F32),
            pltpu.VMEM((40, 128), F32),
            pltpu.VMEM((24, 128), F32),
            pltpu.VMEM((24, 128), F32),
            pltpu.VMEM((4, 8, 128), F32),
            pltpu.VMEM((24, 128), F32),
            pltpu.VMEM((32, 128), F32),
            pltpu.VMEM((24, 128), F32),
            pltpu.VMEM((32, 128), F32),
            pltpu.VMEM((8, 128), F32),
            pltpu.VMEM((3, 128), jnp.int32),
            pltpu.VMEM((27, 16, 128), F32),
            pltpu.VMEM((9, 16, 128), F32),
            pltpu.SMEM((36,), jnp.int32),
            pltpu.SMEM((36,), jnp.int32),
            pltpu.VMEM((19, 8, 16, 128), F32),
            pltpu.VMEM((27, 16, 128), F32),
        ]
        + [
            pltpu.SemaphoreType.DMA(shape)
            for shape in (
                (6, 4), (6, 4), (3, 3), (3, 3), (6, 3), (6, 3), (6, 7), (6, 7), (6,), (3,), (6,), (6,), (4,),
                (3,), (3,), (8,), (8,), (3,), (3,), (5,), (2,),
            )
        ]
    )
    state, moved = pl.pallas_call(
        kernel,
        out_shape=(
            jax.ShapeDtypeStruct((19, 8, 16, 128), F32),
            jax.ShapeDtypeStruct((27, 16, 128), F32),
        ),
        in_specs=[hbm] * 8,
        out_specs=(anywhere, anywhere),
        scratch_shapes=scratch,
        compiler_params=pltpu.CompilerParams(
            collective_id=0, has_side_effects=True, vmem_limit_bytes=48 * 2**20
        ),
        name="remap_and_steps",
    )(*(
        pltpu.with_memory_space_constraint(array, pltpu.HBM)
        for array in (
            old_state.transpose(1, 0, 2),
            send_block,
            receive_slot_table.T,
            interpolation_weight_tiles,
            velocity.reshape(27, 16, 128),
            node_mass,
            spot_x,
            spot_y,
        )
    ))
    return (state, moved.reshape(3, 9, 16, 128))


def solution(mesh):
    return jax.shard_map(
        body,
        mesh=mesh,
        in_specs=(
            P(("gx", "gy"), None, None),
            P(("gx", "gy"), None),
            P(("gx", "gy"), None),
            P(("gx", "gy"), None, None, None),
            P(None, None, "gx", "gy"),
            P(None, "gx", "gy"),
            P(),
            P(),
        ),
        out_specs=(P(None, None, "gx", "gy"), P(None, None, "gx", "gy")),
        check_vma=False,
    )
```

```python
import jax
import jax.numpy as jnp
from jax import lax
from jax.experimental import pallas as pl
from jax.experimental.pallas import tpu as pltpu
from jax.sharding import PartitionSpec as P

SHEAR = 1.0
BULK = 2.0
YIELD_STRESS = 2.0
HARD_ISO = 0.3
HARD_KIN = 0.5
TIME_STEP = 0.2
PEAK_PRESSURE = 1.5
RADIUS_SQUARED = 36.0

MESH = pl.DeviceIdType.MESH
F32 = jnp.float32
BF16 = jnp.bfloat16

ORDERS = (("x", "y", "z"), ("y", "z", "x"), ("z", "x", "y"))
CHUNKS = ((0, 4, 0), (4, 3, 1), (7, 3, 2), (10, 3, 0), (13, 3, 1), (16, 3, 2))
WAVES = ((0, 1, 2), (3, 4, 5))
PIECES = len(CHUNKS)
SPOTS = 36
NODES = 27


def iota(shape, dim):
    return lax.broadcasted_iota(jnp.int32, shape, dim)


def kernel(
    old, sends, asks_in, w, vel_in, mass_in, spot_x_in, spot_y_in,
    state_out, v_out, *scratch,
):
    hbuf, sbuf, ubuf, gbuf = (scratch[n * PIECES:(n + 1) * PIECES] for n in range(4))
    (
        sbuf_in, spread, psel, qsel, xs, wv, rem,
        vext, vcol, dtm, dtmc, press, pressc, ddx, ddy, dsm, s6, fm, cl, cr,
        rowpack, rowin, colpack, colin, corin,
        row_up, row_dn, row_up_in, row_dn_in, cl_in, cr_in, diag_in,
        cr2, row2, cr2_in, row2_in, diag2_in,
        asks, vel, mass, spot_x, spot_y, st, vout,
        p1_s, p1_r, ix_s, ix_r, p2_s, p2_r, p3_s, p3_r, loc1, locx, loc2, loc3, wsem,
        hs, hr, e1_s, e1_r, e2_s, e2_r, load, out_sem,
    ) = scratch[4 * PIECES:]
    di = lax.axis_index("gx")
    dj = lax.axis_index("gy")
    here = {"z": lax.div(di, 2), "c": lax.rem(di, 2), "y": lax.div(dj, 4), "x": lax.rem(dj, 4)}

    def device(**moved):
        at = dict(here)
        for axis, step in moved.items():
            size = 2 if axis == "c" else 4
            at[axis] = lax.rem(at[axis] + step, size)
        return (at["z"] * 2 + at["c"], at["y"] * 4 + at["x"])

    def plate(a, b):
        return (lax.rem(di + (a + 8), 8), lax.rem(dj + (b + 16), 16))

    around = [(a, b) for a in (-1, 0, 1) for b in (-1, 0, 1) if (a, b) != (0, 0)]
    partners = [device(**{axis: d, "c": c}) for axis in "xyz" for d in (1, 2, 3) for c in (0, 1)]
    partners.append(device(c=1))
    partners += [plate(a, b) for a, b in around if b != 0]
    barrier = pltpu.get_barrier_semaphore()
    for partner in partners:
        pl.semaphore_signal(barrier, inc=1, device_id=partner, device_id_type=MESH)

    def remote(src, dst, ssem, rsem, target):
        return pltpu.make_async_remote_copy(
            src_ref=src, dst_ref=dst, send_sem=ssem, recv_sem=rsem, device_id=target, device_id_type=MESH
        )

    local1 = []
    for q, (first, count, order) in enumerate(CHUNKS):
        local1.append(
            pltpu.make_async_copy(old.at[pl.ds(first, count)], hbuf[q].at[here[ORDERS[order][0]]], loc1.at[q])
        )
        local1[q].start()
    localx = []
    for o, (ga, pa, qa) in enumerate(ORDERS):
        localx.append(pltpu.make_async_copy(sends, sbuf_in.at[o, here[ga]], locx.at[o]))
        localx[o].start()
    pairs = ((vel_in, vel), (mass_in, mass), (asks_in, asks), (spot_x_in, spot_x), (spot_y_in, spot_y))
    loads = [pltpu.make_async_copy(src, dst, load.at[n]) for n, (src, dst) in enumerate(pairs)]
    for copy in loads:
        copy.start()
    pl.semaphore_wait(barrier, len(partners))

    phase1 = {}

    def start_phase1(wave):
        for q in wave:
            first, count, order = CHUNKS[q]
            ga = ORDERS[order][0]
            phase1[q] = [
                remote(
                    old.at[pl.ds(first, count)], hbuf[q].at[here[ga]], p1_s.at[q, n], p1_r.at[q, n], device(**{ga: d})
                )
                for n, d in enumerate((1, 3, 2))
            ]
        for n in range(len(phase1[q])):
            for q in wave:
                phase1[q][n].start()

    lists = []
    for d in (1, 2, 3):
        for o, (ga, pa, qa) in enumerate(ORDERS):
            lists.append((o, remote(
                sends, sbuf_in.at[o, here[ga]], ix_s.at[o, d - 1], ix_r.at[o, d - 1], device(**{ga: d})
            )))
            lists[-1][1].start()
    for wave in WAVES:
        start_phase1(wave)

    weights = [
        pltpu.make_async_copy(w.at[pl.ds(n * 32, 32)], wv.at[pl.ds(n * 32, 32)], wsem.at[n]) for n in range(4)
    ]
    for copy in weights:
        copy.start()

    for copy in loads:
        copy.wait()

    lane16 = iota((16, 128), 1)
    packed = jnp.zeros((16, 128), F32)
    for n in range(NODES):
        plane = vel[n]
        rowpack[n:n + 1, :] = plane[0:1, :]
        moved = plane if n == 0 else pltpu.roll(plane, n, 1)
        packed = jnp.where(lane16 == n, moved, packed)
        heavy = pltpu.roll(mass[n % 9], n + 32, 1)
        packed = jnp.where(lane16 == n + 32, heavy, packed)
    colpack[...] = packed
    for n in range(9):
        rowpack[32 + n:33 + n, :] = mass[n, 0:1, :]
    halo = (
        remote(rowpack, rowin, hs.at[0], hr.at[0], plate(-1, 0)),
        remote(colpack, colin, hs.at[1], hr.at[1], plate(0, -1)),
        remote(colpack.at[pl.ds(0, 8)], corin, hs.at[2], hr.at[2], plate(-1, -1)),
    )
    for copy in halo:
        copy.start()

    t192, c768 = iota((192, 128), 0), iota((192, 128), 1)
    aim = (t192 * 10923) >> 16
    part = t192 - aim * 6
    on_p, on_q, on_c = aim >> 3, (aim >> 1) & 3, aim & 1
    for o, (ga, pa, qa) in enumerate(ORDERS):
        at = {ga: here[ga], pa: on_p, qa: on_q}
        stands = (((at["z"] * 2 + on_c) * 4 + at["y"]) * 4 + at["x"]) * 6 + part
        for m in range(6):
            spread[o, :, m * 128:(m + 1) * 128] = jnp.where(stands == c768 + m * 128, 1.0, 0.0).astype(BF16)
    r768 = iota((768, 128), 0)
    sixes = (r768 * 10923) >> 16
    source_of = sixes & 3
    short_row = (sixes >> 2) * 6 + r768 - sixes * 6
    widen = jnp.concatenate(
        [jnp.where(short_row == iota((768, 128), 1) + m, 1.0, 0.0).astype(BF16) for m in (0, 128)], axis=1
    )
    lanes768 = iota((768, 128), 1).astype(F32)

    phase2 = {}

    def selection(o):
        localx[o].wait()
        for of, copy in lists:
            if of == o:
                copy.wait_recv()
        table = jnp.concatenate(
            [sbuf_in[o, n].astype(F32) for n in range(4)] + [jnp.zeros((4, 768), F32)], axis=0
        ).astype(BF16)
        short = lax.dot_general(spread[o], table, (((1,), (1,)), ((), ())), preferred_element_type=F32)
        short = jnp.concatenate([short, jnp.zeros((64, 8), F32)], axis=0).astype(BF16)
        codes = jnp.dot(widen, short, preferred_element_type=F32)
        for sg in range(4):
            hit = (codes[:, sg:sg + 1] == lanes768) & (source_of == sg)
            psel[o, :, sg * 128:(sg + 1) * 128] = jnp.where(hit, 1.0, 0.0).astype(BF16)

    def arrived(q):
        local1[q].wait()
        for copy in phase1[q]:
            copy.wait_recv()

    def start_phase2(q):
        first, count, o = CHUNKS[q]
        ga, pa, qa = ORDERS[o]
        blocks = jnp.concatenate([hbuf[q][:, n].reshape(512, 128) for n in range(count)], axis=1)
        for half in range(2):
            rows = jnp.dot(psel[o, half * 384:(half + 1) * 384, :], blocks, preferred_element_type=F32)
            for t in range(16):
                sbuf[q][half * 2 + t // 8, t % 8] = rows[t * 24:(t + 1) * 24].astype(BF16)
        mine = here[pa]
        own = pltpu.make_async_copy(sbuf[q].at[mine], ubuf[q].at[mine], loc2.at[q])
        own.start()
        copies = [
            remote(sbuf[q].at[lax.rem(mine + d, 4)], ubuf[q].at[mine], p2_s.at[q, d - 1], p2_r.at[q, d - 1], device(**{pa: d}))
            for d in (2, 1, 3)
        ]
        for copy in copies:
            copy.start()
        phase2[q] = (own, copies)

    phase3 = {}

    def start_phase3(q):
        first, count, o = CHUNKS[q]
        ga, pa, qa = ORDERS[o]
        own, copies = phase2[q]
        own.wait()
        for copy in copies:
            copy.wait_recv()
        mine = here[qa] * 2 + here["c"]
        own = pltpu.make_async_copy(ubuf[q].at[:, mine], gbuf[q].at[mine], loc3.at[q])
        own.start()
        copies = []
        for d in (2, 1, 3, 0):
            for c in (0, 1):
                if (d, c) != (0, 0):
                    there = lax.rem(here[qa] + d, 4) * 2 + lax.rem(here["c"] + c, 2)
                    slot = d * 2 + c - 1
                    copies.append(remote(
                        ubuf[q].at[:, there], gbuf[q].at[mine], p3_s.at[q, slot], p3_r.at[q, slot], device(**{qa: d, "c": c})
                    ))
        for copy in copies:
            copy.start()
        phase3[q] = (own, copies)

    def turn(first, last):
        def tile(g, carry):
            for k in range(3):
                wv[g, k] = wv[g, k].T
            return carry

        lax.fori_loop(first, last, tile, 0, unroll=4)

    def arrive(q):
        first, count, o = CHUNKS[q]
        own, copies = phase3[q]
        own.wait()
        for copy in copies:
            copy.wait_recv()
        rows = gbuf[q][...].astype(F32).reshape(768, count * 128).astype(BF16)
        picked = jnp.dot(qsel[o], rows, preferred_element_type=F32)
        for n in range(count):
            xs[pl.ds(first + n, 384, stride=24), :] = picked[:, n * 128:(n + 1) * 128]

    for o in range(3):
        selection(o)
    for q in WAVES[0]:
        arrived(q)
        start_phase2(q)

    asked = asks[...]
    origin = (asked * 10923) >> 16
    slot = asked - origin * 6
    place = {"z": origin >> 5, "c": (origin >> 4) & 1, "y": (origin >> 2) & 3, "x": origin & 3}
    wanted = [
        (((place[qa] * 2 + place["c"]) * 4 + place[pa]) * 24 + place[ga] * 6 + slot).astype(F32) for ga, pa, qa in ORDERS
    ]
    ridx_t = jnp.transpose(jnp.concatenate(wanted + [jnp.zeros((119, 128), F32)], axis=0))
    for q in range(3):
        for k in range(3):
            column = ridx_t[:, q * 3 + k:q * 3 + k + 1]
            for m in range(6):
                hit = column == (iota((128, 128), 1) + m * 128).astype(F32)
                qsel[q, k * 128:(k + 1) * 128, m * 128:(m + 1) * 128] = jnp.where(hit, 1.0, 0.0).astype(BF16)

    row24 = iota((24, 128), 0)
    lane24 = iota((24, 128), 1)
    node_x = (di * 16 + row24).astype(F32)
    node_y = (dj * 128 + lane24).astype(F32)
    next_y = (dj * 128 + 128).astype(F32)

    def spot(n, sums):
        main, side = sums
        sx = spot_x[n].astype(F32)
        sy = spot_y[n].astype(F32)
        far_x = (node_x - sx) ** 2
        main = main + jnp.exp(-(far_x + (node_y - sy) ** 2) / RADIUS_SQUARED)
        side = side + jnp.exp(-(far_x + (next_y - sy) ** 2) / RADIUS_SQUARED)
        return (main, side)

    main, side = lax.fori_loop(0, SPOTS, spot, (jnp.zeros((24, 128), F32), jnp.zeros((24, 128), F32)))
    press[...] = -PEAK_PRESSURE * main
    pressc[...] = jnp.where(lane24 == NODES - 1, -PEAK_PRESSURE * side, 0.0)

    for wave in WAVES[1:]:
        for q in wave:
            arrived(q)
            start_phase2(q)
    for copy in weights:
        copy.wait()
    for q in WAVES[0]:
        start_phase3(q)
    turn(0, 64)
    for q in WAVES[1]:
        start_phase3(q)

    for copy in halo:
        copy.wait_recv()
    low_i, high_i = (di > 0).astype(F32), (di < 7).astype(F32)
    low_j, high_j = (dj > 0).astype(F32), (dj < 15).astype(F32)
    first8 = iota((8, 128), 0) == 0
    row_mask = jnp.where(row24 < 16, 1.0, high_i)
    for n in range(NODES):
        vext[n, 0:16, :] = vel[n]
        vext[n, 16:24, :] = jnp.where(first8, rowin[n:n + 1, :] * high_i, 0.0)
    for n in range(9):
        dtm[n, 0:16, :] = TIME_STEP / mass[n]
        dtm[n, 16:24, :] = jnp.where(first8, high_i * TIME_STEP / rowin[32 + n:33 + n, :], 0.0)
    column = jnp.concatenate([colin[...], jnp.where(first8, corin[...] * high_i, 0.0)], axis=0)
    vcol[...] = jnp.where(lane24 < NODES, column * high_j, 0.0)
    heavy = pltpu.roll(jnp.concatenate([colin[...], corin[...]], axis=0), 96, 1)
    used = (lane24 < NODES) & (row24 < 17)
    dtmc[...] = jnp.where(used, high_j * row_mask * TIME_STEP / jnp.where(used, heavy, 1.0), 0.0)

    def differences():
        edge = lane24 == 127
        for n in range(NODES):
            v = vext[n]
            right = jnp.where(edge, vcol[:, n:n + 1], pltpu.roll(v, 127, 1))
            total = v + right
            delta = right - v
            total_up = pltpu.roll(total, 23, 0)
            delta_up = pltpu.roll(delta, 23, 0)
            ddx[n] = (total_up - total)[0:16]
            ddy[n] = (delta_up + delta)[0:16]
            dsm[n] = (total_up + total)[0:16]

    differences()
    for comp in range(6):
        s6[comp, 0] = jnp.zeros((16, 128), F32)
        s6[comp, 9] = jnp.zeros((16, 128), F32)

    turn(64, 128)
    for wave in WAVES:
        for q in wave:
            arrive(q)

    def block(g, carry):
        parts = [xs[pl.ds(pl.multiple_of((k * 128 + g) * 24, 8), 24), :] for k in range(3)]
        rem[pl.ds(pl.multiple_of(g * 24, 8), 24), :] = jnp.dot(
            jnp.concatenate(parts, axis=1).astype(BF16), wv[g].reshape(384, 128), preferred_element_type=F32
        )
        return carry

    lax.fori_loop(0, 128, block, 0, unroll=16)

    def elements(step):
        def layer(z, carry):
            def state(n):
                if step == 0:
                    return rem[pl.ds(z * 384 + n, 16, stride=24), :]
                return st[n, z]

            gx = [0.25 * (ddx[n * 9 + z] + ddx[n * 9 + z + 1]) for n in range(3)]
            gy = [0.25 * (ddy[n * 9 + z] + ddy[n * 9 + z + 1]) for n in range(3)]
            gz = [0.25 * (dsm[n * 9 + z + 1] - dsm[n * 9 + z]) for n in range(3)]
            strain = [
                TIME_STEP * gx[0],
                TIME_STEP * gy[1],
                TIME_STEP * gz[2],
                TIME_STEP * 0.5 * (gy[0] + gx[1]),
                TIME_STEP * 0.5 * (gz[1] + gy[2]),
                TIME_STEP * 0.5 * (gx[2] + gz[0]),
            ]
            trace = strain[0] + strain[1] + strain[2]
            lame = BULK - 2.0 * SHEAR / 3.0
            trial = []
            for n in range(6):
                value = state(n) + 2.0 * SHEAR * strain[n]
                if n < 3:
                    value = value + lame * trace
                trial.append(value)
            mean = (trial[0] + trial[1] + trial[2]) * (1.0 / 3.0)
            back = [state(6 + n) for n in range(6)]
            xi = [(trial[n] - mean if n < 3 else trial[n]) - back[n] for n in range(6)]
            norm = xi[0] ** 2 + xi[1] ** 2 + xi[2] ** 2 + 2.0 * (xi[3] ** 2 + xi[4] ** 2 + xi[5] ** 2)
            equiv = jnp.sqrt(1.5 * norm)
            epbar = state(18)
            excess = jnp.maximum(equiv - (YIELD_STRESS + HARD_ISO * epbar), 0.0)
            dgamma = excess * (1.0 / (3.0 * SHEAR + HARD_ISO + HARD_KIN))
            factor = dgamma / jnp.maximum(equiv, YIELD_STRESS)
            for n in range(6):
                shift = factor * xi[n]
                stress = trial[n] - 3.0 * SHEAR * shift
                plastic = state(12 + n) + 1.5 * shift
                st[n, z] = stress
                s6[n, z + 1] = stress
                st[6 + n, z] = back[n] + HARD_KIN * shift
                st[12 + n, z] = plastic
            st[18, z] = epbar + dgamma
            return carry

        lax.fori_loop(0, 8, layer, 0)

    along = ((0, 3, 5), (3, 1, 4), (5, 4, 2))
    inner = lane16 > 0
    zeros8 = jnp.zeros((8, 128), F32)

    def forces(last):
        right0 = jnp.zeros((16, 128), F32)
        right1 = jnp.zeros((16, 128), F32)
        left = jnp.zeros((24, 128), F32)
        for i in range(3):
            for k in range(9):
                n = i * 9 + k
                ax = -0.25 * (s6[along[0][i], k + 1] + s6[along[0][i], k])
                ay = -0.25 * (s6[along[1][i], k + 1] + s6[along[1][i], k])
                az = -0.25 * (s6[along[2][i], k] - s6[along[2][i], k + 1])
                near, far = az - ax, az + ax
                near_up, far_up = near + ay, far + ay
                roll0, roll1 = pltpu.roll(near_up, 1, 1), pltpu.roll(far_up, 1, 1)
                e0 = near - ay + jnp.where(inner, roll0, 0.0)
                e1 = far - ay + jnp.where(inner, roll1, 0.0)
                turn0 = roll0 if n == 0 else pltpu.roll(near_up, n + 1, 1)
                turn1 = roll1 if n == 0 else pltpu.roll(far_up, n + 1, 1)
                right0 = jnp.where(lane16 == n, turn0, right0)
                right1 = jnp.where(lane16 == n, turn1, right1)
                whole = jnp.concatenate([e0, zeros8], axis=0) + pltpu.roll(jnp.concatenate([e1, zeros8], axis=0), 1, 0)
                fm[n] = whole
                if last:
                    row2[n:n + 1, :] = whole[16:17]
                else:
                    row_up[n:n + 1, :] = whole[16:17]
                    row_dn[n:n + 1, :] = whole[0:1]
                    left = jnp.where(lane24 == n, whole if n == 0 else pltpu.roll(whole, n, 1), left)
        right = jnp.concatenate([right0, zeros8], axis=0) + pltpu.roll(jnp.concatenate([right1, zeros8], axis=0), 1, 0)
        return left, right

    elements(0)
    left, right = forces(False)
    cl[...] = left
    cr[...] = right
    row_up[32:40, :] = right[16:24]
    row_dn[32:40, :] = right[0:8]
    low, high = pl.ds(0, 8), pl.ds(16, 8)
    round1 = (
        remote(cr.at[high], diag_in.at[0], e1_s.at[4], e1_r.at[4], plate(1, 1)),
        remote(cr.at[low], diag_in.at[1], e1_s.at[5], e1_r.at[5], plate(-1, 1)),
        remote(cl.at[high], diag_in.at[2], e1_s.at[6], e1_r.at[6], plate(1, -1)),
        remote(cl.at[low], diag_in.at[3], e1_s.at[7], e1_r.at[7], plate(-1, -1)),
        remote(cr, cr_in, e1_s.at[2], e1_r.at[2], plate(0, 1)),
        remote(cl, cl_in, e1_s.at[3], e1_r.at[3], plate(0, -1)),
        remote(row_up, row_up_in, e1_s.at[0], e1_r.at[0], plate(1, 0)),
        remote(row_dn, row_dn_in, e1_s.at[1], e1_r.at[1], plate(-1, 0)),
    )
    for copy in round1:
        copy.start()
    for copy in round1:
        copy.wait_recv()

    def ends(at_low, at_high):
        return jnp.concatenate([
            jnp.where(first8, at_low * low_i, 0.0), zeros8, jnp.where(first8, at_high * high_i, 0.0)
        ], axis=0)

    add_left = low_j * (cr_in[...] + ends(diag_in[0], diag_in[1]))
    add_right = high_j * (cl_in[...] + ends(diag_in[2], diag_in[3]))
    col_force = cr[...] + add_right + ends(row_up_in[32:40], row_dn_in[32:40]) + pressc[...]
    vcol[...] = vcol[...] + col_force * dtmc[...]
    for n in range(NODES):
        rows = jnp.concatenate([
            jnp.where(first8, row_up_in[n:n + 1] * low_i, 0.0), zeros8, jnp.where(first8, row_dn_in[n:n + 1] * high_i, 0.0)
        ], axis=0)
        force = fm[n] + rows + jnp.where(lane24 == 0, add_left[:, n:n + 1], 0.0)
        if n == NODES - 1:
            force = force + press[...]
        vext[n] = vext[n] + force * dtm[n % 9]

    differences()
    elements(1)
    left, right = forces(True)
    cr2[...] = right
    round2 = (
        remote(cr2.at[high], diag2_in, e2_s.at[2], e2_r.at[2], plate(1, 1)),
        remote(cr2, cr2_in, e2_s.at[1], e2_r.at[1], plate(0, 1)),
        remote(row2, row2_in, e2_s.at[0], e2_r.at[0], plate(1, 0)),
    )
    for copy in round2:
        copy.start()
    state_copy = pltpu.make_async_copy(st, state_out, out_sem.at[0])
    state_copy.start()
    for copy in round2:
        copy.wait_recv()
    corner = jnp.concatenate([jnp.where(first8, diag2_in[...] * low_i, 0.0), zeros8], axis=0)
    add_left = low_j * (cr2_in[0:16] + corner)
    for n in range(NODES):
        rows = jnp.concatenate([jnp.where(first8, row2_in[n:n + 1] * low_i, 0.0), zeros8], axis=0)
        force = fm[n, 0:16] + rows + jnp.where(lane16 == 0, add_left[:, n:n + 1], 0.0)
        if n == NODES - 1:
            force = force + press[0:16]
        vout[n] = vext[n, 0:16] + force * dtm[n % 9, 0:16]

    v_copy = pltpu.make_async_copy(vout, v_out, out_sem.at[1])
    v_copy.start()
    for o, copy in lists:
        copy.wait_send()
    for q in range(PIECES):
        for copy in phase1[q] + phase2[q][1] + phase3[q][1]:
            copy.wait_send()
    for copy in halo + round1 + round2:
        copy.wait_send()
    state_copy.wait()
    v_copy.wait()


def body(
    old_state,
    send_block,
    receive_slot_table,
    interpolation_weight_tiles,
    velocity,
    node_mass,
    spot_x,
    spot_y,
):
    anywhere = pl.BlockSpec(memory_space=pl.ANY)
    hbm = pl.BlockSpec(memory_space=pltpu.HBM)
    counts = [chunk[1] for chunk in CHUNKS]
    scratch = (
        [pltpu.VMEM((4, n, 128, 128), BF16) for n in counts]
        + [pltpu.VMEM((4, 8, 24, n * 128), BF16) for n in counts]
        + [pltpu.VMEM((4, 8, 24, n * 128), BF16) for n in counts]
        + [pltpu.VMEM((8, 4, 24, n * 128), BF16) for n in counts]
        + [
            pltpu.VMEM((3, 4, 1, 768), jnp.int32),
            pltpu.VMEM((3, 192, 768), BF16),
            pltpu.VMEM((3, 768, 512), BF16),
            pltpu.VMEM((3, 384, 768), BF16),
            pltpu.VMEM((384 * 24, 128), F32),
            pltpu.VMEM((128, 3, 128, 128), BF16),
            pltpu.VMEM((128 * 24, 128), F32),
            pltpu.VMEM((27, 24, 128), F32),
            pltpu.VMEM((24, 128), F32),
            pltpu.VMEM((9, 24, 128), F32),
            pltpu.VMEM((24, 128), F32),
            pltpu.VMEM((24, 128), F32),
            pltpu.VMEM((24, 128), F32),
            pltpu.VMEM((27, 16, 128), F32),
            pltpu.VMEM((27, 16, 128), F32),
            pltpu.VMEM((27, 16, 128), F32),
            pltpu.VMEM((6, 10, 16, 128), F32),
            pltpu.VMEM((27, 24, 128), F32),
            pltpu.VMEM((24, 128), F32),
            pltpu.VMEM((24, 128), F32),
            pltpu.VMEM((48, 128), F32),
            pltpu.VMEM((48, 128), F32),
            pltpu.VMEM((16, 128), F32),
            pltpu.VMEM((16, 128), F32),
            pltpu.VMEM((8, 128), F32),
            pltpu.VMEM((40, 128), F32),
            pltpu.VMEM((40, 128), F32),
            pltpu.VMEM((40, 128), F32),
            pltpu.VMEM((40, 128), F32),
            pltpu.VMEM((24, 128), F32),
            pltpu.VMEM((24, 128), F32),
            pltpu.VMEM((4, 8, 128), F32),
            pltpu.VMEM((24, 128), F32),
            pltpu.VMEM((32, 128), F32),
            pltpu.VMEM((24, 128), F32),
            pltpu.VMEM((32, 128), F32),
            pltpu.VMEM((8, 128), F32),
            pltpu.VMEM((3, 128), jnp.int32),
            pltpu.VMEM((27, 16, 128), F32),
            pltpu.VMEM((9, 16, 128), F32),
            pltpu.SMEM((36,), jnp.int32),
            pltpu.SMEM((36,), jnp.int32),
            pltpu.VMEM((19, 8, 16, 128), F32),
            pltpu.VMEM((27, 16, 128), F32),
        ]
        + [
            pltpu.SemaphoreType.DMA(shape)
            for shape in (
                (6, 3), (6, 3), (3, 3), (3, 3), (6, 3), (6, 3), (6, 7), (6, 7), (6,), (3,), (6,), (6,), (4,),
                (3,), (3,), (8,), (8,), (3,), (3,), (5,), (2,),
            )
        ]
    )
    state, moved = pl.pallas_call(
        kernel,
        out_shape=(
            jax.ShapeDtypeStruct((19, 8, 16, 128), F32),
            jax.ShapeDtypeStruct((27, 16, 128), F32),
        ),
        in_specs=[hbm] * 8,
        out_specs=(anywhere, anywhere),
        scratch_shapes=scratch,
        compiler_params=pltpu.CompilerParams(
            collective_id=0, has_side_effects=True, vmem_limit_bytes=48 * 2**20
        ),
        name="remap_and_steps",
    )(*(
        pltpu.with_memory_space_constraint(array, pltpu.HBM)
        for array in (
            old_state.transpose(1, 0, 2),
            send_block,
            receive_slot_table.T,
            interpolation_weight_tiles,
            velocity.reshape(27, 16, 128),
            node_mass,
            spot_x,
            spot_y,
        )
    ))
    return (state, moved.reshape(3, 9, 16, 128))


def solution(mesh):
    return jax.shard_map(
        body,
        mesh=mesh,
        in_specs=(
            P(("gx", "gy"), None, None),
            P(("gx", "gy"), None),
            P(("gx", "gy"), None),
            P(("gx", "gy"), None, None, None),
            P(None, None, "gx", "gy"),
            P(None, "gx", "gy"),
            P(),
            P(),
        ),
        out_specs=(P(None, None, "gx", "gy"), P(None, None, "gx", "gy")),
        check_vma=False,
    )
```

```python
import jax
import jax.numpy as jnp
from jax import lax
from jax.experimental import pallas as pl
from jax.experimental.pallas import tpu as pltpu
from jax.sharding import PartitionSpec as P

SHEAR = 1.0
BULK = 2.0
YIELD_STRESS = 2.0
HARD_ISO = 0.3
HARD_KIN = 0.5
TIME_STEP = 0.2
PEAK_PRESSURE = 1.5
RADIUS_SQUARED = 36.0

MESH = pl.DeviceIdType.MESH
F32 = jnp.float32
BF16 = jnp.bfloat16

ORDERS = (("x", "y", "z"), ("y", "z", "x"), ("z", "x", "y"))
CHUNKS = ((0, 4, 0), (4, 4, 1), (8, 4, 2), (12, 3, 0), (15, 2, 1), (17, 2, 2))
WAVES = ((0, 1, 2), (3, 4, 5))
PIECES = len(CHUNKS)
SPOTS = 36
NODES = 27


def iota(shape, dim):
    return lax.broadcasted_iota(jnp.int32, shape, dim)


def kernel(
    old, sends, asks_in, w, vel_in, mass_in, spot_x_in, spot_y_in,
    state_out, v_out, *scratch,
):
    hbuf, sbuf, ubuf, gbuf = (scratch[n * PIECES:(n + 1) * PIECES] for n in range(4))
    (
        sbuf_in, spread, psel, qsel, xs, wv, rem,
        vext, vcol, dtm, dtmc, press, pressc, ddx, ddy, dsm, s6, fm, cl, cr,
        rowpack, rowin, colpack, colin, corin,
        row_up, row_dn, row_up_in, row_dn_in, cl_in, cr_in, diag_in,
        cr2, row2, cr2_in, row2_in, diag2_in,
        asks, vel, mass, spot_x, spot_y, st, vout,
        p1_s, p1_r, ix_s, ix_r, p2_s, p2_r, p3_s, p3_r, loc1, locx, loc2, loc3, wsem,
        hs, hr, e1_s, e1_r, e2_s, e2_r, load, out_sem,
    ) = scratch[4 * PIECES:]
    di = lax.axis_index("gx")
    dj = lax.axis_index("gy")
    here = {"z": lax.div(di, 2), "c": lax.rem(di, 2), "y": lax.div(dj, 4), "x": lax.rem(dj, 4)}

    def device(**moved):
        at = dict(here)
        for axis, step in moved.items():
            size = 2 if axis == "c" else 4
            at[axis] = lax.rem(at[axis] + step, size)
        return (at["z"] * 2 + at["c"], at["y"] * 4 + at["x"])

    def plate(a, b):
        return (lax.rem(di + (a + 8), 8), lax.rem(dj + (b + 16), 16))

    around = [(a, b) for a in (-1, 0, 1) for b in (-1, 0, 1) if (a, b) != (0, 0)]
    partners = [device(**{axis: d, "c": c}) for axis in "xyz" for d in (1, 2, 3) for c in (0, 1)]
    partners.append(device(c=1))
    partners += [plate(a, b) for a, b in around if b != 0]
    barrier = pltpu.get_barrier_semaphore()
    for partner in partners:
        pl.semaphore_signal(barrier, inc=1, device_id=partner, device_id_type=MESH)

    def remote(src, dst, ssem, rsem, target):
        return pltpu.make_async_remote_copy(
            src_ref=src, dst_ref=dst, send_sem=ssem, recv_sem=rsem, device_id=target, device_id_type=MESH
        )

    local1 = []
    for q, (first, count, order) in enumerate(CHUNKS):
        local1.append(
            pltpu.make_async_copy(old.at[pl.ds(first, count)], hbuf[q].at[here[ORDERS[order][0]]], loc1.at[q])
        )
        local1[q].start()
    localx = []
    for o, (ga, pa, qa) in enumerate(ORDERS):
        localx.append(pltpu.make_async_copy(sends, sbuf_in.at[o, here[ga]], locx.at[o]))
        localx[o].start()
    pairs = ((vel_in, vel), (mass_in, mass), (asks_in, asks), (spot_x_in, spot_x), (spot_y_in, spot_y))
    loads = [pltpu.make_async_copy(src, dst, load.at[n]) for n, (src, dst) in enumerate(pairs)]
    for copy in loads:
        copy.start()
    pl.semaphore_wait(barrier, len(partners))

    phase1 = {}

    def start_phase1(wave):
        for q in wave:
            first, count, order = CHUNKS[q]
            ga = ORDERS[order][0]
            phase1[q] = [
                remote(
                    old.at[pl.ds(first, count)], hbuf[q].at[here[ga]], p1_s.at[q, n], p1_r.at[q, n], device(**{ga: d})
                )
                for n, d in enumerate((1, 3, 2))
            ]
        for n in range(len(phase1[q])):
            for q in wave:
                phase1[q][n].start()

    lists = []
    for d in (1, 2, 3):
        for o, (ga, pa, qa) in enumerate(ORDERS):
            lists.append((o, remote(
                sends, sbuf_in.at[o, here[ga]], ix_s.at[o, d - 1], ix_r.at[o, d - 1], device(**{ga: d})
            )))
            lists[-1][1].start()
    for wave in WAVES:
        start_phase1(wave)

    weights = [
        pltpu.make_async_copy(w.at[pl.ds(n * 32, 32)], wv.at[pl.ds(n * 32, 32)], wsem.at[n]) for n in range(4)
    ]
    for copy in weights:
        copy.start()

    for copy in loads:
        copy.wait()

    lane16 = iota((16, 128), 1)
    packed = jnp.zeros((16, 128), F32)
    for n in range(NODES):
        plane = vel[n]
        rowpack[n:n + 1, :] = plane[0:1, :]
        moved = plane if n == 0 else pltpu.roll(plane, n, 1)
        packed = jnp.where(lane16 == n, moved, packed)
        heavy = pltpu.roll(mass[n % 9], n + 32, 1)
        packed = jnp.where(lane16 == n + 32, heavy, packed)
    colpack[...] = packed
    for n in range(9):
        rowpack[32 + n:33 + n, :] = mass[n, 0:1, :]
    halo = (
        remote(rowpack, rowin, hs.at[0], hr.at[0], plate(-1, 0)),
        remote(colpack, colin, hs.at[1], hr.at[1], plate(0, -1)),
        remote(colpack.at[pl.ds(0, 8)], corin, hs.at[2], hr.at[2], plate(-1, -1)),
    )
    for copy in halo:
        copy.start()

    t192, c768 = iota((192, 128), 0), iota((192, 128), 1)
    aim = (t192 * 10923) >> 16
    part = t192 - aim * 6
    on_p, on_q, on_c = aim >> 3, (aim >> 1) & 3, aim & 1
    for o, (ga, pa, qa) in enumerate(ORDERS):
        at = {ga: here[ga], pa: on_p, qa: on_q}
        stands = (((at["z"] * 2 + on_c) * 4 + at["y"]) * 4 + at["x"]) * 6 + part
        for m in range(6):
            spread[o, :, m * 128:(m + 1) * 128] = jnp.where(stands == c768 + m * 128, 1.0, 0.0).astype(BF16)
    r768 = iota((768, 128), 0)
    sixes = (r768 * 10923) >> 16
    source_of = sixes & 3
    short_row = (sixes >> 2) * 6 + r768 - sixes * 6
    widen = jnp.concatenate(
        [jnp.where(short_row == iota((768, 128), 1) + m, 1.0, 0.0).astype(BF16) for m in (0, 128)], axis=1
    )
    lanes768 = iota((768, 128), 1).astype(F32)

    phase2 = {}

    def selection(o):
        localx[o].wait()
        for of, copy in lists:
            if of == o:
                copy.wait_recv()
        table = jnp.concatenate(
            [sbuf_in[o, n].astype(F32) for n in range(4)] + [jnp.zeros((4, 768), F32)], axis=0
        ).astype(BF16)
        short = lax.dot_general(spread[o], table, (((1,), (1,)), ((), ())), preferred_element_type=F32)
        short = jnp.concatenate([short, jnp.zeros((64, 8), F32)], axis=0).astype(BF16)
        codes = jnp.dot(widen, short, preferred_element_type=F32)
        for sg in range(4):
            hit = (codes[:, sg:sg + 1] == lanes768) & (source_of == sg)
            psel[o, :, sg * 128:(sg + 1) * 128] = jnp.where(hit, 1.0, 0.0).astype(BF16)

    def arrived(q):
        local1[q].wait()
        for copy in phase1[q]:
            copy.wait_recv()

    def start_phase2(q):
        first, count, o = CHUNKS[q]
        ga, pa, qa = ORDERS[o]
        blocks = jnp.concatenate([hbuf[q][:, n].reshape(512, 128) for n in range(count)], axis=1)
        for half in range(2):
            rows = jnp.dot(psel[o, half * 384:(half + 1) * 384, :], blocks, preferred_element_type=F32)
            for t in range(16):
                sbuf[q][half * 2 + t // 8, t % 8] = rows[t * 24:(t + 1) * 24].astype(BF16)
        mine = here[pa]
        own = pltpu.make_async_copy(sbuf[q].at[mine], ubuf[q].at[mine], loc2.at[q])
        own.start()
        copies = [
            remote(sbuf[q].at[lax.rem(mine + d, 4)], ubuf[q].at[mine], p2_s.at[q, d - 1], p2_r.at[q, d - 1], device(**{pa: d}))
            for d in (2, 1, 3)
        ]
        for copy in copies:
            copy.start()
        phase2[q] = (own, copies)

    phase3 = {}

    def start_phase3(q):
        first, count, o = CHUNKS[q]
        ga, pa, qa = ORDERS[o]
        own, copies = phase2[q]
        own.wait()
        for copy in copies:
            copy.wait_recv()
        mine = here[qa] * 2 + here["c"]
        own = pltpu.make_async_copy(ubuf[q].at[:, mine], gbuf[q].at[mine], loc3.at[q])
        own.start()
        copies = []
        for d in (2, 1, 3, 0):
            for c in (0, 1):
                if (d, c) != (0, 0):
                    there = lax.rem(here[qa] + d, 4) * 2 + lax.rem(here["c"] + c, 2)
                    slot = d * 2 + c - 1
                    copies.append(remote(
                        ubuf[q].at[:, there], gbuf[q].at[mine], p3_s.at[q, slot], p3_r.at[q, slot], device(**{qa: d, "c": c})
                    ))
        for copy in copies:
            copy.start()
        phase3[q] = (own, copies)

    def turn(first, last):
        def tile(g, carry):
            for k in range(3):
                wv[g, k] = wv[g, k].T
            return carry

        lax.fori_loop(first, last, tile, 0, unroll=4)

    def arrive(q):
        first, count, o = CHUNKS[q]
        own, copies = phase3[q]
        own.wait()
        for copy in copies:
            copy.wait_recv()
        rows = gbuf[q][...].astype(F32).reshape(768, count * 128).astype(BF16)
        picked = jnp.dot(qsel[o], rows, preferred_element_type=F32)
        for n in range(count):
            xs[pl.ds(first + n, 384, stride=24), :] = picked[:, n * 128:(n + 1) * 128]

    for o in range(3):
        selection(o)
    for q in WAVES[0]:
        arrived(q)
        start_phase2(q)

    asked = asks[...]
    origin = (asked * 10923) >> 16
    slot = asked - origin * 6
    place = {"z": origin >> 5, "c": (origin >> 4) & 1, "y": (origin >> 2) & 3, "x": origin & 3}
    wanted = [
        (((place[qa] * 2 + place["c"]) * 4 + place[pa]) * 24 + place[ga] * 6 + slot).astype(F32) for ga, pa, qa in ORDERS
    ]
    ridx_t = jnp.transpose(jnp.concatenate(wanted + [jnp.zeros((119, 128), F32)], axis=0))
    for q in range(3):
        for k in range(3):
            column = ridx_t[:, q * 3 + k:q * 3 + k + 1]
            for m in range(6):
                hit = column == (iota((128, 128), 1) + m * 128).astype(F32)
                qsel[q, k * 128:(k + 1) * 128, m * 128:(m + 1) * 128] = jnp.where(hit, 1.0, 0.0).astype(BF16)

    row24 = iota((24, 128), 0)
    lane24 = iota((24, 128), 1)
    node_x = (di * 16 + row24).astype(F32)
    node_y = (dj * 128 + lane24).astype(F32)
    next_y = (dj * 128 + 128).astype(F32)

    def spot(n, sums):
        main, side = sums
        sx = spot_x[n].astype(F32)
        sy = spot_y[n].astype(F32)
        far_x = (node_x - sx) ** 2
        main = main + jnp.exp(-(far_x + (node_y - sy) ** 2) / RADIUS_SQUARED)
        side = side + jnp.exp(-(far_x + (next_y - sy) ** 2) / RADIUS_SQUARED)
        return (main, side)

    main, side = lax.fori_loop(0, SPOTS, spot, (jnp.zeros((24, 128), F32), jnp.zeros((24, 128), F32)))
    press[...] = -PEAK_PRESSURE * main
    pressc[...] = jnp.where(lane24 == NODES - 1, -PEAK_PRESSURE * side, 0.0)

    for wave in WAVES[1:]:
        for q in wave:
            arrived(q)
            start_phase2(q)
    for copy in weights:
        copy.wait()
    for q in WAVES[0]:
        start_phase3(q)
    turn(0, 64)
    for q in WAVES[1]:
        start_phase3(q)

    for copy in halo:
        copy.wait_recv()
    low_i, high_i = (di > 0).astype(F32), (di < 7).astype(F32)
    low_j, high_j = (dj > 0).astype(F32), (dj < 15).astype(F32)
    first8 = iota((8, 128), 0) == 0
    row_mask = jnp.where(row24 < 16, 1.0, high_i)
    for n in range(NODES):
        vext[n, 0:16, :] = vel[n]
        vext[n, 16:24, :] = jnp.where(first8, rowin[n:n + 1, :] * high_i, 0.0)
    for n in range(9):
        dtm[n, 0:16, :] = TIME_STEP / mass[n]
        dtm[n, 16:24, :] = jnp.where(first8, high_i * TIME_STEP / rowin[32 + n:33 + n, :], 0.0)
    column = jnp.concatenate([colin[...], jnp.where(first8, corin[...] * high_i, 0.0)], axis=0)
    vcol[...] = jnp.where(lane24 < NODES, column * high_j, 0.0)
    heavy = pltpu.roll(jnp.concatenate([colin[...], corin[...]], axis=0), 96, 1)
    used = (lane24 < NODES) & (row24 < 17)
    dtmc[...] = jnp.where(used, high_j * row_mask * TIME_STEP / jnp.where(used, heavy, 1.0), 0.0)

    def differences(left_force=None):
        edge = lane24 == 127
        for n in range(NODES):
            v = vext[n]
            if left_force is not None:
                v = v + jnp.where(lane24 == 0, left_force[:, n:n + 1], 0.0) * dtm[n % 9]
                vext[n] = v
            right = jnp.where(edge, vcol[:, n:n + 1], pltpu.roll(v, 127, 1))
            total = v + right
            delta = right - v
            total_up = pltpu.roll(total, 23, 0)
            delta_up = pltpu.roll(delta, 23, 0)
            ddx[n] = (total_up - total)[0:16]
            ddy[n] = (delta_up + delta)[0:16]
            dsm[n] = (total_up + total)[0:16]

    differences()
    for comp in range(6):
        s6[comp, 0] = jnp.zeros((16, 128), F32)
        s6[comp, 9] = jnp.zeros((16, 128), F32)

    turn(64, 128)
    for wave in WAVES:
        for q in wave:
            arrive(q)

    def block(g, carry):
        parts = [xs[pl.ds(pl.multiple_of((k * 128 + g) * 24, 8), 24), :] for k in range(3)]
        rem[pl.ds(pl.multiple_of(g * 24, 8), 24), :] = jnp.dot(
            jnp.concatenate(parts, axis=1).astype(BF16), wv[g].reshape(384, 128), preferred_element_type=F32
        )
        return carry

    lax.fori_loop(0, 128, block, 0, unroll=16)

    def elements(step):
        def layer(z, carry):
            def state(n):
                if step == 0:
                    return rem[pl.ds(z * 384 + n, 16, stride=24), :]
                return st[n, z]

            gx = [0.25 * (ddx[n * 9 + z] + ddx[n * 9 + z + 1]) for n in range(3)]
            gy = [0.25 * (ddy[n * 9 + z] + ddy[n * 9 + z + 1]) for n in range(3)]
            gz = [0.25 * (dsm[n * 9 + z + 1] - dsm[n * 9 + z]) for n in range(3)]
            strain = [
                TIME_STEP * gx[0],
                TIME_STEP * gy[1],
                TIME_STEP * gz[2],
                TIME_STEP * 0.5 * (gy[0] + gx[1]),
                TIME_STEP * 0.5 * (gz[1] + gy[2]),
                TIME_STEP * 0.5 * (gx[2] + gz[0]),
            ]
            trace = strain[0] + strain[1] + strain[2]
            lame = BULK - 2.0 * SHEAR / 3.0
            trial = []
            for n in range(6):
                value = state(n) + 2.0 * SHEAR * strain[n]
                if n < 3:
                    value = value + lame * trace
                trial.append(value)
            mean = (trial[0] + trial[1] + trial[2]) * (1.0 / 3.0)
            back = [state(6 + n) for n in range(6)]
            xi = [(trial[n] - mean if n < 3 else trial[n]) - back[n] for n in range(6)]
            norm = xi[0] ** 2 + xi[1] ** 2 + xi[2] ** 2 + 2.0 * (xi[3] ** 2 + xi[4] ** 2 + xi[5] ** 2)
            equiv = jnp.sqrt(1.5 * norm)
            epbar = state(18)
            excess = jnp.maximum(equiv - (YIELD_STRESS + HARD_ISO * epbar), 0.0)
            dgamma = excess * (1.0 / (3.0 * SHEAR + HARD_ISO + HARD_KIN))
            factor = dgamma / jnp.maximum(equiv, YIELD_STRESS)
            for n in range(6):
                shift = factor * xi[n]
                stress = trial[n] - 3.0 * SHEAR * shift
                plastic = state(12 + n) + 1.5 * shift
                st[n, z] = stress
                s6[n, z + 1] = stress
                st[6 + n, z] = back[n] + HARD_KIN * shift
                st[12 + n, z] = plastic
            st[18, z] = epbar + dgamma
            return carry

        lax.fori_loop(0, 8, layer, 0)

    along = ((0, 3, 5), (3, 1, 4), (5, 4, 2))
    inner = lane16 > 0
    zeros8 = jnp.zeros((8, 128), F32)

    def forces(last):
        right0 = jnp.zeros((16, 128), F32)
        right1 = jnp.zeros((16, 128), F32)
        left = jnp.zeros((24, 128), F32)
        for i in range(3):
            for k in range(9):
                n = i * 9 + k
                ax = -0.25 * (s6[along[0][i], k + 1] + s6[along[0][i], k])
                ay = -0.25 * (s6[along[1][i], k + 1] + s6[along[1][i], k])
                az = -0.25 * (s6[along[2][i], k] - s6[along[2][i], k + 1])
                near, far = az - ax, az + ax
                near_up, far_up = near + ay, far + ay
                roll0, roll1 = pltpu.roll(near_up, 1, 1), pltpu.roll(far_up, 1, 1)
                e0 = near - ay + jnp.where(inner, roll0, 0.0)
                e1 = far - ay + jnp.where(inner, roll1, 0.0)
                turn0 = roll0 if n == 0 else pltpu.roll(near_up, n + 1, 1)
                turn1 = roll1 if n == 0 else pltpu.roll(far_up, n + 1, 1)
                right0 = jnp.where(lane16 == n, turn0, right0)
                right1 = jnp.where(lane16 == n, turn1, right1)
                whole = jnp.concatenate([e0, zeros8], axis=0) + pltpu.roll(jnp.concatenate([e1, zeros8], axis=0), 1, 0)
                fm[n] = whole
                if last:
                    row2[n:n + 1, :] = whole[16:17]
                else:
                    row_up[n:n + 1, :] = whole[16:17]
                    row_dn[n:n + 1, :] = whole[0:1]
                    left = jnp.where(lane24 == n, whole if n == 0 else pltpu.roll(whole, n, 1), left)
        right = jnp.concatenate([right0, zeros8], axis=0) + pltpu.roll(jnp.concatenate([right1, zeros8], axis=0), 1, 0)
        return left, right

    elements(0)
    left, right = forces(False)
    cl[...] = left
    cr[...] = right
    row_up[32:40, :] = right[16:24]
    row_dn[32:40, :] = right[0:8]
    low, high = pl.ds(0, 8), pl.ds(16, 8)
    round1 = (
        remote(cr.at[high], diag_in.at[0], e1_s.at[4], e1_r.at[4], plate(1, 1)),
        remote(cr.at[low], diag_in.at[1], e1_s.at[5], e1_r.at[5], plate(-1, 1)),
        remote(cl.at[high], diag_in.at[2], e1_s.at[6], e1_r.at[6], plate(1, -1)),
        remote(cl.at[low], diag_in.at[3], e1_s.at[7], e1_r.at[7], plate(-1, -1)),
        remote(cr, cr_in, e1_s.at[2], e1_r.at[2], plate(0, 1)),
        remote(cl, cl_in, e1_s.at[3], e1_r.at[3], plate(0, -1)),
        remote(row_up, row_up_in, e1_s.at[0], e1_r.at[0], plate(1, 0)),
        remote(row_dn, row_dn_in, e1_s.at[1], e1_r.at[1], plate(-1, 0)),
    )
    for copy in round1:
        copy.start()
    for copy in round1[6:]:
        copy.wait_recv()
    for n in range(NODES):
        rows = jnp.concatenate([
            jnp.where(first8, row_up_in[n:n + 1] * low_i, 0.0), zeros8, jnp.where(first8, row_dn_in[n:n + 1] * high_i, 0.0)
        ], axis=0)
        force = fm[n] + rows
        if n == NODES - 1:
            force = force + press[...]
        vext[n] = vext[n] + force * dtm[n % 9]
    for copy in round1[:6]:
        copy.wait_recv()

    def ends(at_low, at_high):
        return jnp.concatenate([
            jnp.where(first8, at_low * low_i, 0.0), zeros8, jnp.where(first8, at_high * high_i, 0.0)
        ], axis=0)

    add_left = low_j * (cr_in[...] + ends(diag_in[0], diag_in[1]))
    add_right = high_j * (cl_in[...] + ends(diag_in[2], diag_in[3]))
    col_force = cr[...] + add_right + ends(row_up_in[32:40], row_dn_in[32:40]) + pressc[...]
    vcol[...] = vcol[...] + col_force * dtmc[...]
    differences(add_left)
    elements(1)
    left, right = forces(True)
    cr2[...] = right
    round2 = (
        remote(cr2.at[high], diag2_in, e2_s.at[2], e2_r.at[2], plate(1, 1)),
        remote(cr2, cr2_in, e2_s.at[1], e2_r.at[1], plate(0, 1)),
        remote(row2, row2_in, e2_s.at[0], e2_r.at[0], plate(1, 0)),
    )
    for copy in round2:
        copy.start()
    state_copy = pltpu.make_async_copy(st, state_out, out_sem.at[0])
    state_copy.start()
    for copy in round2:
        copy.wait_recv()
    corner = jnp.concatenate([jnp.where(first8, diag2_in[...] * low_i, 0.0), zeros8], axis=0)
    add_left = low_j * (cr2_in[0:16] + corner)
    for n in range(NODES):
        rows = jnp.concatenate([jnp.where(first8, row2_in[n:n + 1] * low_i, 0.0), zeros8], axis=0)
        force = fm[n, 0:16] + rows + jnp.where(lane16 == 0, add_left[:, n:n + 1], 0.0)
        if n == NODES - 1:
            force = force + press[0:16]
        vout[n] = vext[n, 0:16] + force * dtm[n % 9, 0:16]

    v_copy = pltpu.make_async_copy(vout, v_out, out_sem.at[1])
    v_copy.start()
    for o, copy in lists:
        copy.wait_send()
    for q in range(PIECES):
        for copy in phase1[q] + phase2[q][1] + phase3[q][1]:
            copy.wait_send()
    for copy in halo + round1 + round2:
        copy.wait_send()
    state_copy.wait()
    v_copy.wait()


def body(
    old_state,
    send_block,
    receive_slot_table,
    interpolation_weight_tiles,
    velocity,
    node_mass,
    spot_x,
    spot_y,
):
    anywhere = pl.BlockSpec(memory_space=pl.ANY)
    hbm = pl.BlockSpec(memory_space=pltpu.HBM)
    counts = [chunk[1] for chunk in CHUNKS]
    scratch = (
        [pltpu.VMEM((4, n, 128, 128), BF16) for n in counts]
        + [pltpu.VMEM((4, 8, 24, n * 128), BF16) for n in counts]
        + [pltpu.VMEM((4, 8, 24, n * 128), BF16) for n in counts]
        + [pltpu.VMEM((8, 4, 24, n * 128), BF16) for n in counts]
        + [
            pltpu.VMEM((3, 4, 1, 768), jnp.int32),
            pltpu.VMEM((3, 192, 768), BF16),
            pltpu.VMEM((3, 768, 512), BF16),
            pltpu.VMEM((3, 384, 768), BF16),
            pltpu.VMEM((384 * 24, 128), F32),
            pltpu.VMEM((128, 3, 128, 128), BF16),
            pltpu.VMEM((128 * 24, 128), F32),
            pltpu.VMEM((27, 24, 128), F32),
            pltpu.VMEM((24, 128), F32),
            pltpu.VMEM((9, 24, 128), F32),
            pltpu.VMEM((24, 128), F32),
            pltpu.VMEM((24, 128), F32),
            pltpu.VMEM((24, 128), F32),
            pltpu.VMEM((27, 16, 128), F32),
            pltpu.VMEM((27, 16, 128), F32),
            pltpu.VMEM((27, 16, 128), F32),
            pltpu.VMEM((6, 10, 16, 128), F32),
            pltpu.VMEM((27, 24, 128), F32),
            pltpu.VMEM((24, 128), F32),
            pltpu.VMEM((24, 128), F32),
            pltpu.VMEM((48, 128), F32),
            pltpu.VMEM((48, 128), F32),
            pltpu.VMEM((16, 128), F32),
            pltpu.VMEM((16, 128), F32),
            pltpu.VMEM((8, 128), F32),
            pltpu.VMEM((40, 128), F32),
            pltpu.VMEM((40, 128), F32),
            pltpu.VMEM((40, 128), F32),
            pltpu.VMEM((40, 128), F32),
            pltpu.VMEM((24, 128), F32),
            pltpu.VMEM((24, 128), F32),
            pltpu.VMEM((4, 8, 128), F32),
            pltpu.VMEM((24, 128), F32),
            pltpu.VMEM((32, 128), F32),
            pltpu.VMEM((24, 128), F32),
            pltpu.VMEM((32, 128), F32),
            pltpu.VMEM((8, 128), F32),
            pltpu.VMEM((3, 128), jnp.int32),
            pltpu.VMEM((27, 16, 128), F32),
            pltpu.VMEM((9, 16, 128), F32),
            pltpu.SMEM((36,), jnp.int32),
            pltpu.SMEM((36,), jnp.int32),
            pltpu.VMEM((19, 8, 16, 128), F32),
            pltpu.VMEM((27, 16, 128), F32),
        ]
        + [
            pltpu.SemaphoreType.DMA(shape)
            for shape in (
                (6, 3), (6, 3), (3, 3), (3, 3), (6, 3), (6, 3), (6, 7), (6, 7), (6,), (3,), (6,), (6,), (4,),
                (3,), (3,), (8,), (8,), (3,), (3,), (5,), (2,),
            )
        ]
    )
    state, moved = pl.pallas_call(
        kernel,
        out_shape=(
            jax.ShapeDtypeStruct((19, 8, 16, 128), F32),
            jax.ShapeDtypeStruct((27, 16, 128), F32),
        ),
        in_specs=[hbm] * 8,
        out_specs=(anywhere, anywhere),
        scratch_shapes=scratch,
        compiler_params=pltpu.CompilerParams(
            collective_id=0, has_side_effects=True, vmem_limit_bytes=48 * 2**20
        ),
        name="remap_and_steps",
    )(*(
        pltpu.with_memory_space_constraint(array, pltpu.HBM)
        for array in (
            old_state.transpose(1, 0, 2),
            send_block,
            receive_slot_table.T,
            interpolation_weight_tiles,
            velocity.reshape(27, 16, 128),
            node_mass,
            spot_x,
            spot_y,
        )
    ))
    return (state, moved.reshape(3, 9, 16, 128))


def solution(mesh):
    return jax.shard_map(
        body,
        mesh=mesh,
        in_specs=(
            P(("gx", "gy"), None, None),
            P(("gx", "gy"), None),
            P(("gx", "gy"), None),
            P(("gx", "gy"), None, None, None),
            P(None, None, "gx", "gy"),
            P(None, "gx", "gy"),
            P(),
            P(),
        ),
        out_specs=(P(None, None, "gx", "gy"), P(None, None, "gx", "gy")),
        check_vma=False,
    )
```
